512 devices in a mesh: batch: 32 (over z, core), feat: 16 (over y, x).
Axes of the slice: x: 4, y: 4, z: 16, core: 2. Of those that a mesh axis runs over, the one named last changes fastest.
Arguments:
- vertex_embeddings: bfloat16 [32768, 768], P('batch', 'feat'), may hold values from -6 to 6
- adjacent_vertices: int32 [64, 5, 512, 8], P('batch'), may hold values from -1 to 511
- node_counts: int32 [64], P('batch'), may hold values from 64 to 512, as said below
- target_offsets: int32 [64], P('batch'), may hold values from 0 to 448, as said below
- weight_one: bfloat16 [6, 768, 1024], P(None, 'feat'), may hold values from -0.09375 to 0.09375
- bias_one: float32 [1024], P('feat'), may hold values from -3 to 3
- weight_two: bfloat16 [6, 1024, 153], P(None, 'feat'), may hold values from -0.078125 to 0.078125
- score_derivative: bfloat16 [4096, 153], P('batch'), may hold values from -6 to 6
Outputs:
- logits: float32 [4096, 153], P('batch')
- grad_one: float32 [6, 768, 1024], P(None, 'feat')
- grad_two: float32 [6, 1024, 153], P(None, 'feat')
The draws below stay inside these ranges and needn't reach their ends.
Inputs may be any that keep to these rules, and one draw needn't show every extreme that they name: `node_counts`: in the 2 subgraphs of each index of batch one holds exactly 512 live nodes. `target_offsets`: the 64 targets of a subgraph are live nodes. `adjacent_vertices`: -1 marks an empty slot; slots naming a node at or beyond the subgraph's count, and rows of such nodes, are ignored.
All inputs are finite; a program needn't handle non-finite values.
Results may differ from the reference program's by a relative error of at most 0.012.
The reference program's roundings to bfloat16 on the way count: a program that leaves them out, or rounds other values in their place, can miss the bound.
Values may be sent and summed in bfloat16 or wider, within the bound.
No kernel may reach another device: no remote copies, remote signals or barrier semaphores. Data moves between devices by JAX's collectives and lax.ppermute only.
A program may use at most 64 MiB of HBM per device.

```python
import jax
import jax.numpy as jnp
from jax import lax

EMBEDDING_SIZE = 768
H = 1024
LABEL_CATEGORIES = 153
EDGE_KINDS = 5
ADJACENT_PLACES = 8
SEED_VERTICES = 64
VERTEX_PLACES = 512
GRAPHS_PER_STEP = 2
ALL_SAMPLED_GRAPHS = 64
NODES = 32768
TARGETS = 4096


def pack_counts(key):
    random_seed_amounts, random_seed_whole, random_seed_opening = jax.random.split(key, 3)
    vertical_pieces = ALL_SAMPLED_GRAPHS // GRAPHS_PER_STEP
    sample_vertex_tally = jax.random.randint(random_seed_amounts, (vertical_pieces, GRAPHS_PER_STEP), SEED_VERTICES, VERTEX_PLACES + 1)
    complete_position = jax.random.randint(random_seed_whole, (vertical_pieces, 1), 0, GRAPHS_PER_STEP)
    position_number = jnp.arange(GRAPHS_PER_STEP)[None, :]
    sample_vertex_tally = jnp.where(position_number == complete_position, VERTEX_PLACES, sample_vertex_tally)
    sample_opening_lines = jax.random.randint(random_seed_opening, (vertical_pieces, GRAPHS_PER_STEP), 0, VERTEX_PLACES) % (sample_vertex_tally - SEED_VERTICES + 1)
    sample_opening_lines = jnp.where(position_number == (complete_position + 1) % GRAPHS_PER_STEP, 0, sample_opening_lines)
    sample_opening_lines = jnp.where(position_number == complete_position, VERTEX_PLACES - SEED_VERTICES, sample_opening_lines)
    return (sample_vertex_tally.reshape(ALL_SAMPLED_GRAPHS).astype(jnp.int32), sample_opening_lines.reshape(ALL_SAMPLED_GRAPHS).astype(jnp.int32))


def draw_node_counts(key, part):
    return pack_counts(key)[0]


def draw_target_offsets(key, part):
    return pack_counts(key)[1]


def with_ends(array, rng, least, high):
    shape = array.shape
    index_at = [jax.random.randint(jax.random.fold_in(rng, axis), (), 0, shape[axis]) for axis in range(len(shape))]
    array = array.at[tuple(index_at)].set(least)
    longest = shape.index(max(shape))
    index_at[longest] = (index_at[longest] + 1) % shape[longest]
    return array.at[tuple(index_at)].set(high)


def shard_levels(rng, dims, cuts, least, largest):
    loudness = 1.0
    for dim, parts in cuts:
        steps = jax.random.uniform(jax.random.fold_in(jax.random.fold_in(rng, 6), dim), (parts,), jnp.float32, least / len(cuts), largest / len(cuts))
        loudness = loudness * jnp.repeat(jnp.exp(steps), dims[dim] // parts).reshape((-1,) + (1,) * (len(dims) - 1 - dim))
    return loudness


def scatter_about(key, extent, deviation, reach, pieces=(), kind=jnp.bfloat16):
    result = deviation * jax.random.normal(key, extent, jnp.float32)
    if pieces:
        result = result * shard_levels(key, extent, pieces, -0.22, 0.18)
    return jnp.clip(result, -reach, reach).astype(kind)


def setup_inputs(seed: int = 0) -> dict:
    arg_keys = jax.random.split(jax.random.key(seed), 9)
    vertex_embeddings = scatter_about(arg_keys[0], (NODES, EMBEDDING_SIZE), 1.0, 6.0, ((0, 32), (1, 16)))
    adjacent_vertices = with_ends(jax.random.randint(arg_keys[1], (ALL_SAMPLED_GRAPHS, EDGE_KINDS, VERTEX_PLACES, ADJACENT_PLACES), -1, VERTEX_PLACES), jax.random.fold_in(arg_keys[1], 1), -1, VERTEX_PLACES - 1).astype(jnp.int32)
    node_counts = draw_node_counts(jax.random.fold_in(arg_keys[8], 71), 0)
    target_offsets = draw_target_offsets(jax.random.fold_in(arg_keys[8], 71), 0)
    weight_one = scatter_about(arg_keys[4], (EDGE_KINDS + 1, EMBEDDING_SIZE, H), ((EDGE_KINDS + 1) * EMBEDDING_SIZE) ** -0.5, 0.09375, ((1, 16),))
    bias_one = scatter_about(arg_keys[5], (H,), 0.5, 3.0, ((0, 16),), jnp.float32)
    weight_two = scatter_about(arg_keys[6], (EDGE_KINDS + 1, H, LABEL_CATEGORIES), ((EDGE_KINDS + 1) * H) ** -0.5, 0.078125, ((1, 16),))
    score_derivative = scatter_about(arg_keys[7], (TARGETS, LABEL_CATEGORIES), 1.0, 6.0, ((0, 32),))
    return dict(vertex_embeddings=vertex_embeddings, adjacent_vertices=adjacent_vertices, node_counts=node_counts, target_offsets=target_offsets, weight_one=weight_one, bias_one=bias_one, weight_two=weight_two, score_derivative=score_derivative)


def relation_masks(neighbor_ids, count):
    position = jnp.arange(VERTEX_PLACES, dtype=jnp.int32)
    live_rows = (position < count).astype(jnp.float32)
    adjacency = jnp.zeros((EDGE_KINDS, VERTEX_PLACES, VERTEX_PLACES), jnp.float32)
    for fan_slot in range(ADJACENT_PLACES):
        adjacency = adjacency + (neighbor_ids[:, :, fan_slot, None] == position[None, None, :]).astype(jnp.float32)
    adjacency = adjacency * live_rows[None, :, None] * live_rows[None, None, :]
    degree = jnp.maximum(jnp.sum(adjacency, axis=2), 1.0)
    return adjacency, degree


def reference(vertex_embeddings, adjacent_vertices, node_counts, target_offsets, weight_one, bias_one, weight_two, score_derivative):
    vertex_embedding_lines = vertex_embeddings.reshape(ALL_SAMPLED_GRAPHS, VERTEX_PLACES, EMBEDDING_SIZE)
    derivative_band_pieces = score_derivative.reshape(ALL_SAMPLED_GRAPHS, SEED_VERTICES, LABEL_CATEGORIES)
    weight_first = weight_one.astype(jnp.float32)
    weight_second = weight_two.astype(jnp.float32)

    def one_graph(carry, inputs):
        grad_first, grad_second = carry
        rows_here, neighbor_ids, count, offset, upstream = inputs
        adjacency, degree = relation_masks(neighbor_ids, count)
        mixed = jnp.einsum("rds,sf->rdf", adjacency, rows_here.astype(jnp.float32)) / degree[:, :, None]
        layer_in = jnp.concatenate([rows_here[None], mixed.astype(jnp.bfloat16)], axis=0)
        preact = jnp.einsum("rnf,rfh->nh", layer_in.astype(jnp.float32), weight_first) + bias_one
        hidden_state = jnp.maximum(preact, 0.0).astype(jnp.bfloat16)
        target_adjacency_list = lax.dynamic_slice_in_dim(adjacency, offset, SEED_VERTICES, 1)
        target_deg = lax.dynamic_slice_in_dim(degree, offset, SEED_VERTICES, 1)
        target_hidden = lax.dynamic_slice_in_dim(hidden_state, offset, SEED_VERTICES, 0)
        gathered = jnp.einsum("rts,sh->rth", target_adjacency_list, hidden_state.astype(jnp.float32)) / target_deg[:, :, None]
        second_in = jnp.concatenate([target_hidden[None], gathered.astype(jnp.bfloat16)], axis=0).astype(jnp.float32)
        scores = jnp.einsum("rth,rhc->tc", second_in, weight_second)
        upstream_f = upstream.astype(jnp.float32)
        grad_second = grad_second + jnp.einsum("rth,tc->rhc", second_in, upstream_f)
        returned = jnp.einsum("tc,rhc->rth", upstream_f, weight_second)
        self_part = returned[0].astype(jnp.bfloat16).astype(jnp.float32)
        neighbor_spread = (returned[1:] / target_deg[:, :, None]).astype(jnp.bfloat16).astype(jnp.float32)
        hidden_grad = jnp.einsum("rts,rth->sh", target_adjacency_list, neighbor_spread)
        hidden_grad = hidden_grad + lax.dynamic_update_slice_in_dim(jnp.zeros((VERTEX_PLACES, H), jnp.float32), self_part, offset, 0)
        pre_grad = jnp.where(preact > 0, hidden_grad, 0.0).astype(jnp.bfloat16)
        grad_first = grad_first + jnp.einsum("rnf,nh->rfh", layer_in.astype(jnp.float32), pre_grad.astype(jnp.float32))
        return (grad_first, grad_second), scores

    start = (jnp.zeros((EDGE_KINDS + 1, EMBEDDING_SIZE, H), jnp.float32), jnp.zeros((EDGE_KINDS + 1, H, LABEL_CATEGORIES), jnp.float32))
    (grad_one, grad_two), scores = lax.scan(one_graph, start, (vertex_embedding_lines, adjacent_vertices, node_counts, target_offsets, derivative_band_pieces))
    return scores.reshape(TARGETS, LABEL_CATEGORIES), grad_one, grad_two
```

```python
import jax
import jax.numpy as jnp
from jax import lax
from jax.experimental import pallas as pl
from jax.experimental.pallas import tpu as pltpu
from jax.sharding import PartitionSpec as P

BF16 = jnp.bfloat16
F32 = jnp.float32

GROUPS = 2
CAPACITY = 512
RELATIONS = 5
KINDS = RELATIONS + 1
SLOTS = 8
TARGETS = 64
CLASSES = 153
FEAT = 16
COLUMNS = 48
WIDTH = FEAT * COLUMNS
UNITS = 64
HIDDEN = FEAT * UNITS
PAIRS = KINDS // 2
NODES = GROUPS * CAPACITY
MESSAGE = NODES + KINDS * UNITS
Z = 16
CORES = 2
HALF = COLUMNS // CORES
FIRST_ROWS = PAIRS * HALF
SECOND_ROWS = 16
SHARD_ROWS = FIRST_ROWS + SECOND_ROWS
CLASS_ROWS = 160
VMEM_LIMIT = 56 * 1024 * 1024


def dot(a, b, contract):
    return lax.dot_general(a, b, ((contract[:1], contract[1:]), ((), ())), preferred_element_type=F32)


def eye(size):
    row = lax.broadcasted_iota(jnp.int32, (size, size), 0)
    column = lax.broadcasted_iota(jnp.int32, (size, size), 1)
    return (row == column).astype(F32).astype(BF16)


def swap_halves(tile):
    return pltpu.roll(tile, UNITS, 1)


def low_half(rows):
    return lax.broadcasted_iota(jnp.int32, (rows, 2 * UNITS), 1) < UNITS


def pack_kernel(x_ref, w_ref, out_ref):
    columns = dot(eye(COLUMNS), x_ref[...], (1, 1)).astype(BF16)
    for dest in range(FEAT):
        out_ref[dest, :, :NODES] = columns
    low = low_half(COLUMNS)
    for pair in range(PAIRS):
        for tile in range(FEAT // 2):
            lanes = pl.ds(tile * 2 * UNITS, 2 * UNITS)
            even = w_ref[2 * pair, :, lanes].astype(F32)
            odd = w_ref[2 * pair + 1, :, lanes].astype(F32)
            where = pl.ds(NODES + pair * 2 * UNITS, 2 * UNITS)
            out_ref[2 * tile, :, where] = jnp.where(low, even, swap_halves(odd)).astype(BF16)
            out_ref[2 * tile + 1, :, where] = jnp.where(low, swap_halves(even), odd).astype(BF16)


def layer_kernel(
    counts_ref,
    offsets_ref,
    core_ref,
    message_ref,
    slots_ref,
    bias_ref,
    weight_ref,
    upstream_ref,
    keep_ref,
    send_ref,
    score_ref,
    adj_ref,
    rows_ref,
    mixed_ref,
    low_ref,
    high_ref,
    value_ref,
    whole_ref,
    second_ref,
):
    first_weight = dot(eye(KINDS * UNITS), message_ref[:, NODES:], (1, 1)).astype(BF16)
    node = lax.broadcasted_iota(jnp.int32, (SLOTS, CAPACITY), 1)
    tile_row = lax.broadcasted_iota(jnp.int32, (16, CAPACITY), 0).astype(F32).astype(BF16)
    one = jnp.ones((16, CAPACITY), BF16)
    zero = jnp.zeros((16, CAPACITY), BF16)
    target = lax.broadcasted_iota(jnp.int32, (TARGETS, CAPACITY), 0)
    place = lax.broadcasted_iota(jnp.int32, (TARGETS, CAPACITY), 1)
    half = CAPACITY // 2
    for group in range(GROUPS):
        count = counts_ref[group]
        offset = offsets_ref[group]
        lanes = slice(group * CAPACITY, (group + 1) * CAPACITY)
        pick = (place == target + offset).astype(F32).astype(BF16)
        rows_ref[:TARGETS, :] = pick

        def relation_step(relation, carry, group=group, count=count, lanes=lanes, pick=pick):
            ids = slots_ref[group, relation]
            live = (ids >= 0) & (ids < count) & (node < count)
            inverse = 1.0 / jnp.maximum(jnp.sum(live.astype(F32), axis=0, keepdims=True), 1.0)
            for part in range(2):
                inside = live & (ids >= part * half) & (ids < (part + 1) * half)
                value = jnp.where(inside, ids - part * half, -1).astype(F32)
                for slot in range(SLOTS):
                    value_ref[part, slot] = jnp.broadcast_to(
                        value[slot : slot + 1, :], (16, CAPACITY)
                    ).astype(BF16)
            for part in range(2):

                def tile_step(step, carry, part=part):
                    base = step * 32
                    here = tile_row + base.astype(F32).astype(BF16)
                    there = here + jnp.full((), 16, BF16)
                    first = zero
                    second = zero
                    for slot in range(SLOTS):
                        value = value_ref[part, slot]
                        first = first + jnp.where(value == here, one, zero)
                        second = second + jnp.where(value == there, one, zero)
                    start = pl.multiple_of(part * half + base, 32)
                    adj_ref[pl.ds(start, 16), :] = first
                    adj_ref[pl.ds(start + 16, 16), :] = second
                    return carry

                lax.fori_loop(0, half // 32, tile_step, 0)
            adjacency = adj_ref[...]
            for block in range(3):
                size = WIDTH // 3
                mixed = dot(message_ref[block * size : (block + 1) * size, lanes], adjacency, (1, 0))
                start = pl.multiple_of(relation * WIDTH + block * size, size)
                mixed_ref[group, pl.ds(start, size), :] = (mixed * inverse).astype(BF16)
            start = pl.multiple_of((relation + 1) * TARGETS, TARGETS)
            rows_ref[pl.ds(start, TARGETS), :] = dot(pick, adjacency, (1, 1)).astype(BF16)
            return carry

        lax.fori_loop(0, RELATIONS, relation_step, 0)

        preact = bias_ref[...] + dot(first_weight[:UNITS], message_ref[:, lanes], (1, 0))
        for kind in range(1, KINDS):
            preact = preact + dot(
                first_weight[kind * UNITS : (kind + 1) * UNITS],
                mixed_ref[group, (kind - 1) * WIDTH : kind * WIDTH, :],
                (1, 0),
            )
        hidden = jnp.maximum(preact, 0.0).astype(BF16)
        rows = rows_ref[...]
        degree = jnp.maximum(jnp.sum(rows.astype(F32), axis=1, keepdims=True), 1.0)
        second_in = (dot(rows, hidden, (1, 1)) / degree).astype(BF16)
        upstream = upstream_ref[group * TARGETS : (group + 1) * TARGETS, :]
        scores = jnp.zeros((TARGETS, CLASSES), F32)
        returned = []
        for kind in range(KINDS):
            piece = slice(kind * TARGETS, (kind + 1) * TARGETS)
            scores = scores + dot(second_in[piece], weight_ref[kind], (1, 0))
            returned.append(dot(upstream, weight_ref[kind], (1, 1)))
        score_ref[group * TARGETS : (group + 1) * TARGETS, :] = scores
        spread = (jnp.concatenate(returned, axis=0) / degree).astype(BF16)
        wide = jnp.concatenate(
            [second_in[kind * TARGETS : (kind + 1) * TARGETS].astype(F32) for kind in range(KINDS)], axis=1
        ).astype(BF16)
        grad_second = dot(upstream, wide, (0, 0))
        if group == 0:
            second_ref[...] = grad_second
        else:
            second_ref[...] += grad_second
        hidden_grad = dot(spread, rows, (0, 0))
        pre_grad = jnp.where(preact > 0, hidden_grad, 0.0)
        nothing = jnp.zeros_like(pre_grad)
        low_ref[group] = jnp.concatenate([pre_grad, nothing], axis=0).astype(BF16)
        high_ref[group] = jnp.concatenate([nothing, pre_grad], axis=0).astype(BF16)

    for pair in range(PAIRS):
        total = jnp.zeros((WIDTH, 2 * UNITS), F32)
        for group in range(GROUPS):
            lanes = slice(group * CAPACITY, (group + 1) * CAPACITY)
            if pair == 0:
                even = message_ref[:, lanes]
            else:
                even = mixed_ref[group, (2 * pair - 1) * WIDTH : 2 * pair * WIDTH, :]
            odd = mixed_ref[group, 2 * pair * WIDTH : (2 * pair + 1) * WIDTH, :]
            total = total + dot(even, low_ref[group], (1, 1)) + dot(odd, high_ref[group], (1, 1))
        total = total.reshape(FEAT, COLUMNS, 2 * UNITS)
        for part in range(CORES):
            whole_ref[part, :, pair * HALF : (pair + 1) * HALF, :] = total[:, part * HALF : (part + 1) * HALF, :]
    tail = jnp.zeros((CLASS_ROWS - CLASSES, 2 * UNITS), F32)
    packed = []
    for pair in range(PAIRS):
        packed.append(second_ref[:, pair * 2 * UNITS : (pair + 1) * 2 * UNITS])
        packed.append(tail)
    packed.append(jnp.zeros((Z * CORES * SECOND_ROWS - PAIRS * CLASS_ROWS, 2 * UNITS), F32))
    packed = jnp.concatenate(packed, axis=0).reshape(Z, CORES, SECOND_ROWS, 2 * UNITS)
    for part in range(CORES):
        whole_ref[part, :, FIRST_ROWS:, :] = packed[:, part]
    core = core_ref[0]
    keep_ref[...] = whole_ref[core]
    send_ref[...] = whole_ref[1 - core]


def unpack_kernel(shards_ref, first_ref, second_ref):
    low = low_half(HALF)
    for tile in range(FEAT // 2):
        lanes = pl.ds(tile * 2 * UNITS, 2 * UNITS)
        for part in range(CORES):
            left = shards_ref[(2 * tile) * CORES + part].astype(F32)
            right = shards_ref[(2 * tile + 1) * CORES + part].astype(F32)
            rows = pl.ds(part * HALF, HALF)
            for pair in range(PAIRS):
                a = left[pair * HALF : (pair + 1) * HALF]
                b = right[pair * HALF : (pair + 1) * HALF]
                first_ref[2 * pair, rows, lanes] = jnp.where(low, a, swap_halves(b))
                first_ref[2 * pair + 1, rows, lanes] = jnp.where(low, swap_halves(a), b)
    packed = shards_ref[...].astype(F32)[:, FIRST_ROWS:, :].reshape(Z * CORES * SECOND_ROWS, 2 * UNITS)
    identity = eye(2 * UNITS)
    for pair in range(PAIRS):
        block = packed[pair * CLASS_ROWS : (pair + 1) * CLASS_ROWS].astype(BF16)
        turned = dot(identity, block, (1, 1))
        second_ref[2 * pair] = turned[:UNITS, :CLASSES]
        second_ref[2 * pair + 1] = turned[UNITS:, :CLASSES]


VMEM = pl.BlockSpec(memory_space=pltpu.VMEM)
SMEM = pl.BlockSpec(memory_space=pltpu.SMEM)
PARAMS = pltpu.CompilerParams(vmem_limit_bytes=VMEM_LIMIT)


def pack(x, w):
    return pl.pallas_call(
        pack_kernel,
        out_shape=jax.ShapeDtypeStruct((FEAT, COLUMNS, MESSAGE), BF16),
        in_specs=[VMEM, VMEM],
        out_specs=VMEM,
        compiler_params=PARAMS,
    )(x, w)


def layers(counts, offsets, core, message, slots, bias, weight, upstream):
    shard = jax.ShapeDtypeStruct((Z, SHARD_ROWS, 2 * UNITS), F32)
    return pl.pallas_call(
        layer_kernel,
        out_shape=(shard, shard, jax.ShapeDtypeStruct((GROUPS * TARGETS, CLASSES), F32)),
        in_specs=[SMEM, SMEM, SMEM, VMEM, VMEM, VMEM, VMEM, VMEM],
        out_specs=(VMEM, VMEM, VMEM),
        scratch_shapes=[
            pltpu.VMEM((CAPACITY, CAPACITY), BF16),
            pltpu.VMEM((KINDS * TARGETS, CAPACITY), BF16),
            pltpu.VMEM((GROUPS, RELATIONS * WIDTH, CAPACITY), BF16),
            pltpu.VMEM((GROUPS, 2 * UNITS, CAPACITY), BF16),
            pltpu.VMEM((GROUPS, 2 * UNITS, CAPACITY), BF16),
            pltpu.VMEM((2, SLOTS, 16, CAPACITY), BF16),
            pltpu.VMEM((CORES, Z, SHARD_ROWS, 2 * UNITS), F32),
            pltpu.VMEM((CLASSES, KINDS * UNITS), F32),
        ],
        compiler_params=PARAMS,
    )(counts, offsets, core, message, slots, bias, weight, upstream)


def unpack(shards):
    return pl.pallas_call(
        unpack_kernel,
        out_shape=(
            jax.ShapeDtypeStruct((KINDS, COLUMNS, HIDDEN), F32),
            jax.ShapeDtypeStruct((KINDS, UNITS, CLASSES), F32),
        ),
        in_specs=[VMEM],
        out_specs=(VMEM, VMEM),
        compiler_params=PARAMS,
    )(shards)


def local(
    vertex_embeddings,
    adjacent_vertices,
    node_counts,
    target_offsets,
    weight_one,
    bias_one,
    weight_two,
    score_derivative,
):
    batch = lax.axis_index("batch")
    core = (batch % CORES).astype(jnp.int32).reshape(1)
    slots = jnp.swapaxes(adjacent_vertices, 2, 3)
    message = lax.all_to_all(pack(vertex_embeddings, weight_one), "feat", 0, 0)
    message = message.reshape(WIDTH, MESSAGE)
    keep, send, partial_scores = layers(
        node_counts,
        target_offsets,
        core,
        message,
        slots,
        bias_one.reshape(UNITS, 1),
        weight_two,
        score_derivative,
    )
    scores = jnp.sum(lax.all_gather(partial_scores, "feat"), axis=0)
    received = lax.ppermute(send, "batch", [(i, i ^ 1) for i in range(Z * CORES)])
    chip = keep + received
    first = lax.all_to_all(chip[:, :FIRST_ROWS].astype(BF16), "feat", 0, 0)
    shards = jnp.concatenate([first, chip[:, FIRST_ROWS:].astype(BF16)], axis=1)
    same_core = [[z * CORES + c for z in range(Z)] for c in range(CORES)]
    pieces = lax.all_to_all(shards, "batch", 0, 0, axis_index_groups=same_core)
    shard = jnp.sum(pieces.astype(F32), axis=0).astype(BF16)
    first_grad, second_grad = unpack(lax.all_gather(shard, "batch"))
    return (scores, first_grad, second_grad)


def solution(mesh):
    placed = (
        P("batch", "feat"),
        P("batch", None, None, None),
        P("batch"),
        P("batch"),
        P(None, "feat", None),
        P("feat"),
        P(None, "feat", None),
        P("batch", None),
    )
    return jax.shard_map(
        local,
        mesh=mesh,
        in_specs=placed,
        out_specs=(P("batch", None), P(None, "feat", None), P(None, "feat", None)),
        check_vma=False,
    )
```

```python
import jax
import jax.numpy as jnp
from jax import lax
from jax.experimental import pallas as pl
from jax.experimental.pallas import tpu as pltpu
from jax.sharding import PartitionSpec as P

BF16 = jnp.bfloat16
F32 = jnp.float32

GROUPS = 2
CAPACITY = 512
RELATIONS = 5
KINDS = RELATIONS + 1
SLOTS = 8
TARGETS = 64
CLASSES = 153
FEAT = 16
COLUMNS = 48
WIDTH = FEAT * COLUMNS
UNITS = 64
HIDDEN = FEAT * UNITS
PAIRS = KINDS // 2
NODES = GROUPS * CAPACITY
WEIGHT_LANES = 256
MESSAGE = NODES + WEIGHT_LANES
Z = 16
CORES = 2
HALF = COLUMNS // CORES
FIRST_ROWS = PAIRS * HALF
SECOND_ROWS = 16
SHARD_ROWS = SECOND_ROWS + FIRST_ROWS
CLASS_ROWS = 160
SIDE = 4
CLASS_PART = CLASS_ROWS // SIDE
SCORE_ROWS = 48
ADJ_ROWS = RELATIONS * CAPACITY
ROWS = KINDS * TARGETS
MIB = 1024 * 1024


def dot(a, b, contract):
    return lax.dot_general(a, b, ((contract[:1], contract[1:]), ((), ())), preferred_element_type=F32)


def eye(size):
    row = lax.broadcasted_iota(jnp.int32, (size, size), 0)
    column = lax.broadcasted_iota(jnp.int32, (size, size), 1)
    return (row == column).astype(F32).astype(BF16)


def swap_halves(tile):
    return pltpu.roll(tile, UNITS, 1)


def low_half(rows):
    return lax.broadcasted_iota(jnp.int32, (rows, 2 * UNITS), 1) < UNITS


def pack_kernel(core_ref, x_ref, w_ref, out_ref):
    columns = x_ref[...]
    for dest in range(FEAT):
        out_ref[dest, :, :NODES] = columns
    low = low_half(COLUMNS)
    core = core_ref[0]
    for tile in range(FEAT // 2):
        lanes = pl.ds(tile * 2 * UNITS, 2 * UNITS)
        first, second, third = [w_ref[2 * pair + core, :, lanes].astype(F32) for pair in range(PAIRS)]
        front = pl.ds(NODES, 2 * UNITS)
        back = pl.ds(NODES + 2 * UNITS, 2 * UNITS)
        out_ref[2 * tile, :, front] = jnp.where(low, first, swap_halves(second)).astype(BF16)
        out_ref[2 * tile, :, back] = third.astype(BF16)
        out_ref[2 * tile + 1, :, front] = jnp.where(low, swap_halves(first), second).astype(BF16)
        out_ref[2 * tile + 1, :, back] = swap_halves(third).astype(BF16)


def live_slots(ids, count):
    node = lax.broadcasted_iota(jnp.int32, (SLOTS, CAPACITY), 1)
    return (ids >= 0) & (ids < count) & (node < count)


def adjacency_kernel(counts_ref, offsets_ref, slots_ref, adj_ref, value_ref):
    tile_row = lax.broadcasted_iota(jnp.int32, (16, CAPACITY), 0).astype(F32).astype(BF16)
    one = jnp.ones((16, CAPACITY), BF16)
    zero = jnp.zeros((16, CAPACITY), BF16)
    target = lax.broadcasted_iota(jnp.int32, (TARGETS, CAPACITY), 0)
    place = lax.broadcasted_iota(jnp.int32, (TARGETS, CAPACITY), 1)
    half = CAPACITY // 2
    for group in range(GROUPS):
        count = counts_ref[group]
        pick = (place == target + offsets_ref[group]).astype(F32).astype(BF16)
        adj_ref[group, ADJ_ROWS : ADJ_ROWS + TARGETS, :] = pick

        def relation_step(relation, carry, group=group, count=count, pick=pick):
            ids = slots_ref[group, relation]
            live = live_slots(ids, count)
            origin = pl.multiple_of(relation * CAPACITY, CAPACITY)
            for part in range(2):
                inside = live & (ids >= part * half) & (ids < (part + 1) * half)
                value = jnp.where(inside, ids - part * half, -1).astype(F32)
                for slot in range(SLOTS):
                    value_ref[part, slot] = jnp.broadcast_to(
                        value[slot : slot + 1, :], (16, CAPACITY)
                    ).astype(BF16)
            for part in range(2):

                def tile_step(step, carry, part=part):
                    base = step * 32
                    here = tile_row + base.astype(F32).astype(BF16)
                    there = here + jnp.full((), 16, BF16)
                    first = zero
                    second = zero
                    for slot in range(SLOTS):
                        value = value_ref[part, slot]
                        first = first + jnp.where(value == here, one, zero)
                        second = second + jnp.where(value == there, one, zero)
                    start = pl.multiple_of(origin + part * half + base, 32)
                    adj_ref[group, pl.ds(start, 16), :] = first
                    adj_ref[group, pl.ds(start + 16, 16), :] = second
                    return carry

                lax.fori_loop(0, half // 32, tile_step, 0)
            start = pl.multiple_of(ADJ_ROWS + (relation + 1) * TARGETS, TARGETS)
            adj_ref[group, pl.ds(start, TARGETS), :] = dot(
                pick, adj_ref[group, pl.ds(origin, CAPACITY), :], (1, 1)
            ).astype(BF16)
            return carry

        lax.fori_loop(0, RELATIONS, relation_step, 0)


def layer_kernel(
    core_ref,
    counts_ref,
    message_ref,
    first_ref,
    slots_ref,
    bias_ref,
    weight_ref,
    upstream_ref,
    adj_from,
    keep_ref,
    send_ref,
    score_ref,
    adj_ref,
    adj_sem,
    mixed_ref,
    low_ref,
    high_ref,
    whole_ref,
    second_ref,
):
    def fetch(group, relation):
        rows = pl.ds(pl.multiple_of(relation * CAPACITY, CAPACITY), CAPACITY)
        return pltpu.make_async_copy(
            adj_from.at[group, rows], adj_ref.at[group, rows], adj_sem.at[group, relation]
        )

    def fetch_rows(group):
        rows = pl.ds(ADJ_ROWS, ROWS)
        return pltpu.make_async_copy(
            adj_from.at[group, rows], adj_ref.at[group, rows], adj_sem.at[group, RELATIONS]
        )

    for group in range(GROUPS):
        for relation in range(RELATIONS):
            fetch(group, relation).start()
        fetch_rows(group).start()
    turn = eye(WEIGHT_LANES)
    first_weight = [dot(turn, first_ref[part], (1, 1)).astype(BF16) for part in range(CORES)]
    size = WIDTH // 3
    score_parts = []
    for group in range(GROUPS):
        lanes = slice(group * CAPACITY, (group + 1) * CAPACITY)

        count = counts_ref[group]

        def relation_step(relation, carry, group=group, lanes=lanes, count=count):
            fetch(group, relation).wait()
            rows = pl.ds(pl.multiple_of(relation * CAPACITY, CAPACITY), CAPACITY)
            adjacency = adj_ref[group, rows, :]
            live = live_slots(slots_ref[group, relation], count)
            inverse = 1.0 / jnp.maximum(jnp.sum(live.astype(F32), axis=0, keepdims=True), 1.0)
            for block in range(3):
                mixed = dot(message_ref[block * size : (block + 1) * size, lanes], adjacency, (1, 0))
                start = pl.multiple_of(relation * WIDTH + block * size, size)
                mixed_ref[group, pl.ds(start, size), :] = (mixed * inverse).astype(BF16)
            return carry

        lax.fori_loop(0, RELATIONS, relation_step, 0)

        preact = bias_ref[...] + dot(first_weight[0][:UNITS], message_ref[:, lanes], (1, 0))
        for kind in range(1, KINDS):
            preact = preact + dot(
                first_weight[kind % CORES][kind // CORES * UNITS : (kind // CORES + 1) * UNITS],
                mixed_ref[group, (kind - 1) * WIDTH : kind * WIDTH, :],
                (1, 0),
            )
        hidden = jnp.maximum(preact, 0.0).astype(BF16)
        fetch_rows(group).wait()
        rows = adj_ref[group, ADJ_ROWS:, :]
        degree = jnp.maximum(jnp.sum(rows.astype(F32), axis=1, keepdims=True), 1.0)
        second_in = (dot(rows, hidden, (1, 1)) / degree).astype(BF16)
        upstream = upstream_ref[group * TARGETS : (group + 1) * TARGETS, :]
        returned = []
        for kind in range(KINDS):
            returned.append(dot(upstream, weight_ref[kind * UNITS : (kind + 1) * UNITS, :], (1, 1)))
        spread = (jnp.concatenate(returned, axis=0) / degree).astype(BF16)
        wide = jnp.concatenate(
            [second_in[kind * TARGETS : (kind + 1) * TARGETS].astype(F32) for kind in range(KINDS)], axis=1
        ).astype(BF16)
        score_parts.append(dot(weight_ref[...], wide, (0, 1)))
        grad_second = dot(upstream, wide, (0, 0))
        if group == 0:
            second_ref[...] = grad_second
        else:
            second_ref[...] += grad_second
        hidden_grad = dot(spread, rows, (0, 0))
        pre_grad = jnp.where(preact > 0, hidden_grad, 0.0)
        nothing = jnp.zeros_like(pre_grad)
        low_ref[group] = jnp.concatenate([pre_grad, nothing], axis=0).astype(BF16)
        high_ref[group] = jnp.concatenate([nothing, pre_grad], axis=0).astype(BF16)

    tail = jnp.zeros((CLASS_ROWS - CLASSES, 2 * UNITS), F32)
    score = jnp.concatenate([jnp.concatenate(score_parts, axis=1), tail], axis=0)
    for part in range(SIDE):
        piece = score[part * CLASS_PART : (part + 1) * CLASS_PART]
        piece = jnp.concatenate([piece, jnp.zeros((SCORE_ROWS - CLASS_PART, 2 * UNITS), F32)], axis=0)
        score_ref[part] = piece.astype(BF16)
    for pair in range(PAIRS):
        total = jnp.zeros((WIDTH, 2 * UNITS), F32)
        for group in range(GROUPS):
            lanes = slice(group * CAPACITY, (group + 1) * CAPACITY)
            if pair == 0:
                even = message_ref[:, lanes]
            else:
                even = mixed_ref[group, (2 * pair - 1) * WIDTH : 2 * pair * WIDTH, :]
            odd = mixed_ref[group, 2 * pair * WIDTH : (2 * pair + 1) * WIDTH, :]
            total = total + dot(even, low_ref[group], (1, 1)) + dot(odd, high_ref[group], (1, 1))
        total = total.reshape(FEAT, COLUMNS, 2 * UNITS)
        start = SECOND_ROWS + pair * HALF
        for part in range(CORES):
            whole_ref[part, :, start : start + HALF, :] = total[:, part * HALF : (part + 1) * HALF, :]
    packed = []
    for pair in range(PAIRS):
        packed.append(second_ref[:, pair * 2 * UNITS : (pair + 1) * 2 * UNITS])
        packed.append(tail)
    packed.append(jnp.zeros((Z * CORES * SECOND_ROWS - PAIRS * CLASS_ROWS, 2 * UNITS), F32))
    packed = jnp.concatenate(packed, axis=0).reshape(Z, CORES, SECOND_ROWS, 2 * UNITS)
    for part in range(CORES):
        whole_ref[part, :, :SECOND_ROWS, :] = packed[:, part]
    core = core_ref[0]
    keep_ref[...] = whole_ref[core]
    send_ref[...] = whole_ref[1 - core]


def merge_kernel(keep_ref, received_ref, score_ref, message_ref, second_ref):
    chip = keep_ref[...] + received_ref[...]
    message_ref[:, SCORE_ROWS:, :] = chip[:, SECOND_ROWS:, :].astype(BF16)
    for part in range(FEAT):
        message_ref[part, :SCORE_ROWS, :] = score_ref[part % SIDE]
    second_ref[...] = chip[:, :SECOND_ROWS, :].astype(BF16)


def relay_kernel(message_ref, second_ref, shards_ref):
    shards_ref[:, SECOND_ROWS:, :] = message_ref[:, SCORE_ROWS:, :]
    shards_ref[:, :SECOND_ROWS, :] = second_ref[...]


def score_kernel(message_ref, score_ref):
    total = message_ref[0, :SCORE_ROWS, :].astype(F32)
    for part in range(1, FEAT):
        total = total + message_ref[part, :SCORE_ROWS, :].astype(F32)
    score_ref[...] = total[:CLASS_PART]


def unpack_kernel(place_ref, shards_ref, s0_ref, s1_ref, s2_ref, s3_ref, first_ref, second_ref, logits_ref, scores_ref):
    low = low_half(HALF)
    for tile in range(FEAT // 2):
        lanes = pl.ds(tile * 2 * UNITS, 2 * UNITS)
        for part in range(CORES):
            left = shards_ref[(2 * tile) * CORES + part].astype(F32)
            right = shards_ref[(2 * tile + 1) * CORES + part].astype(F32)
            rows = pl.ds(part * HALF, HALF)
            for pair in range(PAIRS):
                start = SECOND_ROWS + pair * HALF
                a = left[start : start + HALF]
                b = right[start : start + HALF]
                first_ref[2 * pair, rows, lanes] = jnp.where(low, a, swap_halves(b))
                first_ref[2 * pair + 1, rows, lanes] = jnp.where(low, swap_halves(a), b)
    packed = shards_ref[:, :SECOND_ROWS, :].reshape(Z * CORES * SECOND_ROWS, 2 * UNITS)
    identity = eye(2 * UNITS)
    for pair in range(PAIRS):
        block = packed[pair * CLASS_ROWS : (pair + 1) * CLASS_ROWS]
        turned = dot(identity, block, (1, 1))
        second_ref[2 * pair] = turned[:UNITS, :CLASSES]
        second_ref[2 * pair + 1] = turned[UNITS:, :CLASSES]
    for step, ref in enumerate((s0_ref, s1_ref, s2_ref, s3_ref)):
        part = (place_ref[0] + SIDE - step) % SIDE
        scores_ref[pl.ds(pl.multiple_of(part * CLASS_PART, 8), CLASS_PART), :] = ref[...]
    logits_ref[...] = scores_ref[:CLASSES, :]


VMEM = pl.BlockSpec(memory_space=pltpu.VMEM)
SMEM = pl.BlockSpec(memory_space=pltpu.SMEM)


def params(mib):
    return pltpu.CompilerParams(vmem_limit_bytes=mib * MIB)


def cost(flops, size):
    return pl.CostEstimate(flops=flops, bytes_accessed=size, transcendentals=0)


def shape(*dims, dtype=BF16):
    return jax.ShapeDtypeStruct(dims, dtype)


def pack(core, x, w):
    return pl.pallas_call(
        pack_kernel,
        out_shape=shape(FEAT, COLUMNS, MESSAGE),
        in_specs=[SMEM, VMEM, VMEM],
        out_specs=VMEM,
        compiler_params=params(58),
    )(core, x, w)


def adjacency(counts, offsets, slots):
    return pl.pallas_call(
        adjacency_kernel,
        out_shape=shape(GROUPS, ADJ_ROWS + ROWS, CAPACITY),
        in_specs=[SMEM, SMEM, VMEM],
        out_specs=VMEM,
        scratch_shapes=[pltpu.VMEM((2, SLOTS, 16, CAPACITY), BF16)],
        compiler_params=params(58),
        cost_estimate=cost(8 * 10**9, 8 * MIB),
    )(counts, offsets, slots)


def layers(core, counts, message, first, slots, bias, weight, upstream, adj):
    shard = shape(Z, SHARD_ROWS, 2 * UNITS, dtype=F32)
    return pl.pallas_call(
        layer_kernel,
        out_shape=(shard, shard, shape(SIDE, SCORE_ROWS, 2 * UNITS)),
        in_specs=[SMEM] * 2 + [VMEM] * 6 + [pl.BlockSpec(memory_space=pl.ANY)],
        out_specs=(VMEM, VMEM, VMEM),
        scratch_shapes=[
            pltpu.VMEM(adj.shape, BF16),
            pltpu.SemaphoreType.DMA((GROUPS, KINDS)),
            pltpu.VMEM((GROUPS, RELATIONS * WIDTH, CAPACITY), BF16),
            pltpu.VMEM((GROUPS, 2 * UNITS, CAPACITY), BF16),
            pltpu.VMEM((GROUPS, 2 * UNITS, CAPACITY), BF16),
            pltpu.VMEM((CORES, Z, SHARD_ROWS, 2 * UNITS), F32),
            pltpu.VMEM((CLASSES, KINDS * UNITS), F32),
        ],
        compiler_params=params(44),
        cost_estimate=cost(12 * 10**9, 12 * MIB),
    )(core, counts, message, first, slots, bias, weight, upstream, adj)


def merge(keep, received, score):
    return pl.pallas_call(
        merge_kernel,
        out_shape=(shape(FEAT, SCORE_ROWS + FIRST_ROWS, 2 * UNITS), shape(Z, SECOND_ROWS, 2 * UNITS)),
        in_specs=[VMEM] * 3,
        out_specs=(VMEM, VMEM),
        compiler_params=params(8),
    )(keep, received, score)


def relay(message, second):
    return pl.pallas_call(
        relay_kernel,
        out_shape=shape(Z, SHARD_ROWS, 2 * UNITS),
        in_specs=[VMEM] * 2,
        out_specs=VMEM,
        compiler_params=params(8),
    )(message, second)


def add_scores(message):
    return pl.pallas_call(
        score_kernel,
        out_shape=shape(CLASS_PART, 2 * UNITS, dtype=F32),
        in_specs=[VMEM],
        out_specs=VMEM,
        compiler_params=params(8),
        cost_estimate=cost(2 * 10**9, 2 * MIB),
    )(message)


def gather_scores(score):
    parts = [score]
    for step in range(1, SIDE):
        hops = [(i, i // SIDE * SIDE + (i + step) % SIDE) for i in range(FEAT)]
        parts.append(lax.ppermute(score, "feat", hops))
    return parts


def unpack(place, shards, blocks):
    return pl.pallas_call(
        unpack_kernel,
        out_shape=(
            shape(KINDS, COLUMNS, HIDDEN, dtype=F32),
            shape(KINDS, UNITS, CLASSES, dtype=F32),
            shape(CLASSES, GROUPS * TARGETS, dtype=F32),
        ),
        in_specs=[SMEM] + [VMEM] * 5,
        out_specs=(VMEM, VMEM, VMEM),
        scratch_shapes=[pltpu.VMEM((CLASS_ROWS, 2 * UNITS), F32)],
        compiler_params=params(8),
    )(place, shards, *blocks)


def local(
    vertex_embeddings,
    adjacent_vertices,
    node_counts,
    target_offsets,
    weight_one,
    bias_one,
    weight_two,
    score_derivative,
):
    core = (lax.axis_index("batch") % CORES).astype(jnp.int32).reshape(1)
    place = (lax.axis_index("feat") % SIDE).astype(jnp.int32).reshape(1)
    chips = [[z * CORES + c for c in range(CORES)] for z in range(Z)]
    same_core = [[z * CORES + c for z in range(Z)] for c in range(CORES)]
    message = lax.all_to_all(pack(core, vertex_embeddings.T, weight_one), "feat", 0, 0)
    message = message.reshape(WIDTH, MESSAGE)
    first = lax.all_gather(message[:, NODES:], "batch", axis_index_groups=chips)
    slots = jnp.swapaxes(adjacent_vertices, 2, 3)
    adj = adjacency(node_counts, target_offsets, slots)
    keep, send, score = layers(
        core,
        node_counts,
        message,
        first,
        slots,
        bias_one.reshape(UNITS, 1),
        weight_two.reshape(KINDS * UNITS, CLASSES),
        score_derivative,
        adj,
    )
    received = lax.ppermute(send, "batch", [(i, i ^ 1) for i in range(Z * CORES)])
    first, second = merge(keep, received, score)
    first = lax.all_to_all(first, "feat", 0, 0)
    shards = relay(first, second)
    pieces = lax.all_to_all(shards, "batch", 0, 0, axis_index_groups=same_core)
    blocks = gather_scores(add_scores(first))
    shard = jnp.sum(pieces.astype(F32), axis=0).astype(BF16)
    first_grad, second_grad, logits = unpack(place, lax.all_gather(shard, "batch"), blocks)
    return (logits.T, first_grad, second_grad)


def solution(mesh):
    placed = (
        P("batch", "feat"),
        P("batch", None, None, None),
        P("batch"),
        P("batch"),
        P(None, "feat", None),
        P("feat"),
        P(None, "feat", None),
        P("batch", None),
    )
    return jax.shard_map(
        local,
        mesh=mesh,
        in_specs=placed,
        out_specs=(P("batch", None), P(None, "feat", None), P(None, "feat", None)),
        check_vma=False,
    )
```

```python
import jax
import jax.numpy as jnp
from jax import lax
from jax.experimental import pallas as pl
from jax.experimental.pallas import tpu as pltpu
from jax.sharding import PartitionSpec as P

BF16 = jnp.bfloat16
F32 = jnp.float32

GROUPS = 2
CAPACITY = 512
RELATIONS = 5
KINDS = RELATIONS + 1
SLOTS = 8
TARGETS = 64
CLASSES = 153
FEAT = 16
COLUMNS = 48
WIDTH = FEAT * COLUMNS
UNITS = 64
HIDDEN = FEAT * UNITS
PAIRS = KINDS // 2
NODES = GROUPS * CAPACITY
WEIGHT_LANES = 256
MESSAGE = NODES + WEIGHT_LANES
Z = 16
CORES = 2
HALF = COLUMNS // CORES
FIRST_ROWS = PAIRS * HALF
SECOND_ROWS = 16
SHARD_ROWS = SECOND_ROWS + FIRST_ROWS
CLASS_ROWS = 160
SIDE = 4
ADJ_ROWS = RELATIONS * CAPACITY
ROWS = KINDS * TARGETS
MIB = 1024 * 1024


def dot(a, b, contract):
    return lax.dot_general(a, b, ((contract[:1], contract[1:]), ((), ())), preferred_element_type=F32)


def eye(size):
    row = lax.broadcasted_iota(jnp.int32, (size, size), 0)
    column = lax.broadcasted_iota(jnp.int32, (size, size), 1)
    return (row == column).astype(F32).astype(BF16)


def swap_halves(tile):
    return pltpu.roll(tile, UNITS, 1)


def low_half(rows):
    return lax.broadcasted_iota(jnp.int32, (rows, 2 * UNITS), 1) < UNITS


def pack_kernel(core_ref, x_ref, w_ref, out_ref):
    columns = x_ref[...]
    for dest in range(FEAT):
        out_ref[dest, :, :NODES] = columns
    low = low_half(COLUMNS)
    core = core_ref[0]
    for tile in range(FEAT // 2):
        lanes = pl.ds(tile * 2 * UNITS, 2 * UNITS)
        first, second, third = [w_ref[2 * pair + core, :, lanes].astype(F32) for pair in range(PAIRS)]
        front = pl.ds(NODES, 2 * UNITS)
        back = pl.ds(NODES + 2 * UNITS, 2 * UNITS)
        out_ref[2 * tile, :, front] = jnp.where(low, first, swap_halves(second)).astype(BF16)
        out_ref[2 * tile, :, back] = third.astype(BF16)
        out_ref[2 * tile + 1, :, front] = jnp.where(low, swap_halves(first), second).astype(BF16)
        out_ref[2 * tile + 1, :, back] = swap_halves(third).astype(BF16)


def live_slots(ids, count):
    node = lax.broadcasted_iota(jnp.int32, (SLOTS, CAPACITY), 1)
    return (ids >= 0) & (ids < count) & (node < count)


def adjacency_kernel(
    counts_ref,
    offsets_ref,
    slots_ref,
    weight_ref,
    upstream_ref,
    adj_ref,
    grad_ref,
    degree_ref,
    value_ref,
):
    tile_row = lax.broadcasted_iota(jnp.int32, (16, CAPACITY), 0).astype(F32).astype(BF16)
    one = jnp.ones((16, CAPACITY), BF16)
    zero = jnp.zeros((16, CAPACITY), BF16)
    target = lax.broadcasted_iota(jnp.int32, (TARGETS, CAPACITY), 0)
    place = lax.broadcasted_iota(jnp.int32, (TARGETS, CAPACITY), 1)
    half = CAPACITY // 2
    for group in range(GROUPS):
        count = counts_ref[group]
        pick = (place == target + offsets_ref[group]).astype(F32).astype(BF16)
        adj_ref[group, ADJ_ROWS : ADJ_ROWS + TARGETS, :] = pick

        def relation_step(relation, carry, group=group, count=count, pick=pick):
            ids = slots_ref[group, relation]
            live = live_slots(ids, count)
            origin = pl.multiple_of(relation * CAPACITY, CAPACITY)
            for part in range(2):
                inside = live & (ids >= part * half) & (ids < (part + 1) * half)
                value = jnp.where(inside, ids - part * half, -1).astype(F32)
                for slot in range(SLOTS):
                    value_ref[part, slot] = jnp.broadcast_to(
                        value[slot : slot + 1, :], (16, CAPACITY)
                    ).astype(BF16)
            for part in range(2):

                def tile_step(step, carry, part=part):
                    base = step * 32
                    here = tile_row + base.astype(F32).astype(BF16)
                    there = here + jnp.full((), 16, BF16)
                    first = zero
                    second = zero
                    for slot in range(SLOTS):
                        value = value_ref[part, slot]
                        first = first + jnp.where(value == here, one, zero)
                        second = second + jnp.where(value == there, one, zero)
                    start = pl.multiple_of(origin + part * half + base, 32)
                    adj_ref[group, pl.ds(start, 16), :] = first
                    adj_ref[group, pl.ds(start + 16, 16), :] = second
                    return carry

                lax.fori_loop(0, half // 32, tile_step, 0)
            start = pl.multiple_of(ADJ_ROWS + (relation + 1) * TARGETS, TARGETS)
            adj_ref[group, pl.ds(start, TARGETS), :] = dot(
                pick, adj_ref[group, pl.ds(origin, CAPACITY), :], (1, 1)
            ).astype(BF16)
            return carry

        lax.fori_loop(0, RELATIONS, relation_step, 0)
        rows = adj_ref[group, ADJ_ROWS:, :]
        degree = jnp.maximum(jnp.sum(rows.astype(F32), axis=1, keepdims=True), 1.0)
        degree_ref[group] = jnp.broadcast_to(degree, (ROWS, 2 * UNITS))
        upstream = upstream_ref[group * TARGETS : (group + 1) * TARGETS, :]
        returned = []
        for kind in range(KINDS):
            returned.append(dot(upstream, weight_ref[kind * UNITS : (kind + 1) * UNITS, :], (1, 1)))
        spread = (jnp.concatenate(returned, axis=0) / degree).astype(BF16)
        grad_ref[group] = dot(spread, rows, (0, 0))


def layer_kernel(
    core_ref,
    counts_ref,
    message_ref,
    first_ref,
    slots_ref,
    bias_ref,
    weight_ref,
    upstream_ref,
    adj_from,
    grad_from,
    degree_from,
    keep_ref,
    send_ref,
    score_ref,
    adj_ref,
    grad_ref,
    degree_ref,
    adj_sem,
    other_sem,
    mixed_ref,
    low_ref,
    high_ref,
    whole_ref,
):
    def fetch(group, relation):
        size = CAPACITY if relation < RELATIONS else ROWS
        rows = pl.ds(relation * CAPACITY, size)
        return pltpu.make_async_copy(
            adj_from.at[group, rows], adj_ref.at[group, rows], adj_sem.at[group, relation]
        )

    others = [
        pltpu.make_async_copy(grad_from, grad_ref, other_sem.at[0]),
        pltpu.make_async_copy(degree_from, degree_ref, other_sem.at[1]),
    ]
    for group in range(GROUPS):
        for relation in range(KINDS):
            fetch(group, relation).start()
        if group == 0:
            others[0].start()
            others[1].start()
    turn = eye(WEIGHT_LANES)
    first_weight = [dot(turn, first_ref[part], (1, 1)).astype(BF16) for part in range(CORES)]
    size = WIDTH // 3
    preacts = []
    for group in range(GROUPS):
        lanes = slice(group * CAPACITY, (group + 1) * CAPACITY)
        count = counts_ref[group]
        for relation in range(RELATIONS):
            fetch(group, relation).wait()
            adjacency = adj_ref[group, relation * CAPACITY : (relation + 1) * CAPACITY, :]
            live = live_slots(slots_ref[group, relation], count)
            inverse = 1.0 / jnp.maximum(jnp.sum(live.astype(F32), axis=0, keepdims=True), 1.0)
            for block in range(3):
                mixed = dot(message_ref[block * size : (block + 1) * size, lanes], adjacency, (1, 0))
                start = relation * WIDTH + block * size
                mixed_ref[group, start : start + size, :] = (mixed * inverse).astype(BF16)
        preact = bias_ref[...] + dot(first_weight[0][:UNITS], message_ref[:, lanes], (1, 0))
        for kind in range(1, KINDS):
            preact = preact + dot(
                first_weight[kind % CORES][kind // CORES * UNITS : (kind // CORES + 1) * UNITS],
                mixed_ref[group, (kind - 1) * WIDTH : kind * WIDTH, :],
                (1, 0),
            )
        preacts.append(preact)
    others[0].wait()
    others[1].wait()
    hiddens = []
    for group, preact in enumerate(preacts):
        hiddens.append(jnp.maximum(preact, 0.0).astype(BF16))
        pre_grad = jnp.where(preact > 0, grad_ref[group], 0.0)
        nothing = jnp.zeros_like(pre_grad)
        low_ref[group] = jnp.concatenate([pre_grad, nothing], axis=0).astype(BF16)
        high_ref[group] = jnp.concatenate([nothing, pre_grad], axis=0).astype(BF16)
    score_parts = []
    grad_second = jnp.zeros((CLASSES, KINDS * UNITS), F32)
    for group, hidden in enumerate(hiddens):
        fetch(group, RELATIONS).wait()
        rows = adj_ref[group, ADJ_ROWS:, :]
        second_in = dot(rows, hidden, (1, 1)) / degree_ref[group][:, :UNITS]
        wide = jnp.concatenate(
            [second_in[kind * TARGETS : (kind + 1) * TARGETS] for kind in range(KINDS)], axis=1
        ).astype(BF16)
        score_parts.append(dot(weight_ref[...], wide, (0, 1)))
        upstream = upstream_ref[group * TARGETS : (group + 1) * TARGETS, :]
        grad_second = grad_second + dot(upstream, wide, (0, 0))
    tail = jnp.zeros((CLASS_ROWS - CLASSES, 2 * UNITS), F32)
    score = jnp.concatenate([jnp.concatenate(score_parts, axis=1), tail], axis=0)
    score_ref[...] = score
    for pair in range(PAIRS):
        total = jnp.zeros((WIDTH, 2 * UNITS), F32)
        for group in range(GROUPS):
            lanes = slice(group * CAPACITY, (group + 1) * CAPACITY)
            if pair == 0:
                even = message_ref[:, lanes]
            else:
                even = mixed_ref[group, (2 * pair - 1) * WIDTH : 2 * pair * WIDTH, :]
            odd = mixed_ref[group, 2 * pair * WIDTH : (2 * pair + 1) * WIDTH, :]
            total = total + dot(even, low_ref[group], (1, 1)) + dot(odd, high_ref[group], (1, 1))
        total = total.reshape(FEAT, COLUMNS, 2 * UNITS)
        start = SECOND_ROWS + pair * HALF
        for part in range(CORES):
            whole_ref[part, :, start : start + HALF, :] = total[:, part * HALF : (part + 1) * HALF, :]
    packed = []
    for pair in range(PAIRS):
        packed.append(grad_second[:, pair * 2 * UNITS : (pair + 1) * 2 * UNITS])
        packed.append(tail)
    packed.append(jnp.zeros((Z * CORES * SECOND_ROWS - PAIRS * CLASS_ROWS, 2 * UNITS), F32))
    packed = jnp.concatenate(packed, axis=0).reshape(Z, CORES, SECOND_ROWS, 2 * UNITS)
    for part in range(CORES):
        whole_ref[part, :, :SECOND_ROWS, :] = packed[:, part]
    core = core_ref[0]
    keep_ref[...] = whole_ref[core]
    send_ref[...] = whole_ref[1 - core]


def merge_kernel(keep_ref, received_ref, message_ref, second_ref):
    chip = keep_ref[...] + received_ref[...]
    message_ref[...] = chip[:, SECOND_ROWS:, :].astype(BF16)
    second_ref[...] = chip[:, :SECOND_ROWS, :].astype(BF16)


def relay_kernel(message_ref, second_ref, score_ref, shards_ref, passed_ref):
    shards_ref[:, SECOND_ROWS:, :] = message_ref[...]
    shards_ref[:, :SECOND_ROWS, :] = second_ref[...]
    passed_ref[...] = score_ref[...]


def fold_kernel(pieces_ref, s0_ref, s1_ref, s2_ref, s3_ref, copies_ref, score_ref):
    total = pieces_ref[0].astype(F32)
    for part in range(1, Z):
        total = total + pieces_ref[part].astype(F32)
    total = total.astype(BF16)
    for part in range(Z):
        copies_ref[part] = total
    score_ref[...] = s0_ref[...] + s1_ref[...] + s2_ref[...] + s3_ref[...]


def unpack_kernel(shards_ref, s0_ref, s1_ref, s2_ref, s3_ref, first_ref, second_ref, logits_ref):
    low = low_half(HALF)
    for tile in range(FEAT // 2):
        lanes = pl.ds(tile * 2 * UNITS, 2 * UNITS)
        for part in range(CORES):
            left = shards_ref[part, 2 * tile].astype(F32)
            right = shards_ref[part, 2 * tile + 1].astype(F32)
            rows = pl.ds(part * HALF, HALF)
            for pair in range(PAIRS):
                start = SECOND_ROWS + pair * HALF
                a = left[start : start + HALF]
                b = right[start : start + HALF]
                first_ref[2 * pair, rows, lanes] = jnp.where(low, a, swap_halves(b))
                first_ref[2 * pair + 1, rows, lanes] = jnp.where(low, swap_halves(a), b)
    packed = jnp.stack([shards_ref[part, :, :SECOND_ROWS, :] for part in range(CORES)], axis=1)
    packed = packed.reshape(Z * CORES * SECOND_ROWS, 2 * UNITS)
    identity = eye(2 * UNITS)
    for pair in range(PAIRS):
        block = packed[pair * CLASS_ROWS : (pair + 1) * CLASS_ROWS]
        turned = dot(identity, block, (1, 1))
        second_ref[2 * pair] = turned[:UNITS, :CLASSES]
        second_ref[2 * pair + 1] = turned[UNITS:, :CLASSES]
    logits_ref[...] = (s0_ref[...] + s1_ref[...] + s2_ref[...] + s3_ref[...])[:CLASSES]


VMEM = pl.BlockSpec(memory_space=pltpu.VMEM)
SMEM = pl.BlockSpec(memory_space=pltpu.SMEM)


def params(mib):
    return pltpu.CompilerParams(vmem_limit_bytes=mib * MIB)


def cost(flops, size):
    return pl.CostEstimate(flops=flops, bytes_accessed=size, transcendentals=0)


def shape(*dims, dtype=BF16):
    return jax.ShapeDtypeStruct(dims, dtype)


def pack(core, x, w):
    return pl.pallas_call(
        pack_kernel,
        out_shape=shape(FEAT, COLUMNS, MESSAGE),
        in_specs=[SMEM, VMEM, VMEM],
        out_specs=VMEM,
        compiler_params=params(58),
    )(core, x, w)


def adjacency(counts, offsets, slots, weight, upstream):
    return pl.pallas_call(
        adjacency_kernel,
        out_shape=(
            shape(GROUPS, ADJ_ROWS + ROWS, CAPACITY),
            shape(GROUPS, UNITS, CAPACITY, dtype=F32),
            shape(GROUPS, ROWS, 2 * UNITS, dtype=F32),
        ),
        in_specs=[SMEM] * 2 + [VMEM] * 3,
        out_specs=(VMEM,) * 3,
        scratch_shapes=[pltpu.VMEM((2, SLOTS, 16, CAPACITY), BF16)],
        compiler_params=params(58),
        cost_estimate=cost(8 * 10**9, 8 * MIB),
    )(counts, offsets, slots, weight, upstream)


def layers(core, counts, message, first, slots, bias, weight, upstream, adj, grad, degree):
    shard = shape(Z, SHARD_ROWS, 2 * UNITS, dtype=F32)
    return pl.pallas_call(
        layer_kernel,
        out_shape=(shard, shard, shape(CLASS_ROWS, GROUPS * TARGETS, dtype=F32)),
        in_specs=[SMEM] * 2 + [VMEM] * 6 + [pl.BlockSpec(memory_space=pl.ANY)] * 3,
        out_specs=(VMEM, VMEM, VMEM),
        scratch_shapes=[
            pltpu.VMEM(adj.shape, BF16),
            pltpu.VMEM(grad.shape, F32),
            pltpu.VMEM(degree.shape, F32),
            pltpu.SemaphoreType.DMA((GROUPS, KINDS)),
            pltpu.SemaphoreType.DMA((2,)),
            pltpu.VMEM((GROUPS, RELATIONS * WIDTH, CAPACITY), BF16),
            pltpu.VMEM((GROUPS, 2 * UNITS, CAPACITY), BF16),
            pltpu.VMEM((GROUPS, 2 * UNITS, CAPACITY), BF16),
            pltpu.VMEM((CORES, Z, SHARD_ROWS, 2 * UNITS), F32),
        ],
        compiler_params=params(44),
        cost_estimate=cost(12 * 10**9, 12 * MIB),
    )(core, counts, message, first, slots, bias, weight, upstream, adj, grad, degree)


def merge(keep, received):
    return pl.pallas_call(
        merge_kernel,
        out_shape=(shape(FEAT, FIRST_ROWS, 2 * UNITS), shape(Z, SECOND_ROWS, 2 * UNITS)),
        in_specs=[VMEM] * 2,
        out_specs=(VMEM,) * 2,
        compiler_params=params(8),
    )(keep, received)


def relay(message, second, score):
    return pl.pallas_call(
        relay_kernel,
        out_shape=(shape(Z, SHARD_ROWS, 2 * UNITS), shape(*score.shape, dtype=F32)),
        in_specs=[VMEM] * 3,
        out_specs=(VMEM,) * 2,
        compiler_params=params(8),
    )(message, second, score)


def fold(pieces, scores):
    return pl.pallas_call(
        fold_kernel,
        out_shape=(shape(Z, SHARD_ROWS, 2 * UNITS), shape(*scores[0].shape, dtype=F32)),
        in_specs=[VMEM] * 5,
        out_specs=(VMEM,) * 2,
        compiler_params=params(8),
    )(pieces, *scores)


def row_hops(step):
    return [(i, i // SIDE * SIDE + (i + step) % SIDE) for i in range(FEAT)]


def column_hops(step):
    return [(i, (i + step * SIDE) % FEAT) for i in range(FEAT)]


def spread_out(score, hops):
    return [score] + [lax.ppermute(score, "feat", hops(step)) for step in range(1, SIDE)]


def unpack(shards, scores):
    return pl.pallas_call(
        unpack_kernel,
        out_shape=(
            shape(KINDS, COLUMNS, HIDDEN, dtype=F32),
            shape(KINDS, UNITS, CLASSES, dtype=F32),
            shape(CLASSES, GROUPS * TARGETS, dtype=F32),
        ),
        in_specs=[VMEM] * 5,
        out_specs=(VMEM, VMEM, VMEM),
        compiler_params=params(8),
    )(shards, *scores)


def local(
    vertex_embeddings,
    adjacent_vertices,
    node_counts,
    target_offsets,
    weight_one,
    bias_one,
    weight_two,
    score_derivative,
):
    core = (lax.axis_index("batch") % CORES).astype(jnp.int32).reshape(1)
    chips = [[z * CORES + c for c in range(CORES)] for z in range(Z)]
    same_core = [[z * CORES + c for z in range(Z)] for c in range(CORES)]
    message = lax.all_to_all(pack(core, vertex_embeddings.T, weight_one), "feat", 0, 0)
    message = message.reshape(WIDTH, MESSAGE)
    first = lax.all_gather(message[:, NODES:], "batch", axis_index_groups=chips)
    slots = jnp.swapaxes(adjacent_vertices, 2, 3)
    weight = weight_two.reshape(KINDS * UNITS, CLASSES)
    adj, grad, degree = adjacency(node_counts, target_offsets, slots, weight, score_derivative)
    keep, send, score = layers(
        core,
        node_counts,
        message,
        first,
        slots,
        bias_one.reshape(UNITS, 1),
        weight,
        score_derivative,
        adj,
        grad,
        degree,
    )
    received = lax.ppermute(send, "batch", [(i, i ^ 1) for i in range(Z * CORES)])
    message, second = merge(keep, received)
    message = lax.all_to_all(message, "feat", 0, 0)
    shards, score = relay(message, second, score)
    pieces = lax.all_to_all(shards, "batch", 0, 0, axis_index_groups=same_core)
    copies, score = fold(pieces, spread_out(score, row_hops))
    shards = lax.all_to_all(copies, "batch", 0, 0, axis_index_groups=same_core)
    scores = spread_out(score, column_hops)
    shards = lax.all_gather(shards, "batch", axis_index_groups=chips)
    first_grad, second_grad, logits = unpack(shards, scores)
    return (logits.T, first_grad, second_grad)


def solution(mesh):
    placed = (
        P("batch", "feat"),
        P("batch", None, None, None),
        P("batch"),
        P("batch"),
        P(None, "feat", None),
        P("feat"),
        P(None, "feat", None),
        P("batch", None),
    )
    return jax.shard_map(
        local,
        mesh=mesh,
        in_specs=placed,
        out_specs=(P("batch", None), P(None, "feat", None), P(None, "feat", None)),
        check_vma=False,
    )
```

```python
import jax
import jax.numpy as jnp
from jax import lax
from jax.experimental import pallas as pl
from jax.experimental.pallas import tpu as pltpu
from jax.sharding import PartitionSpec as P

BF16 = jnp.bfloat16
F32 = jnp.float32

GROUPS = 2
CAPACITY = 512
RELATIONS = 5
KINDS = RELATIONS + 1
SLOTS = 8
TARGETS = 64
CLASSES = 153
FEAT = 16
COLUMNS = 48
WIDTH = FEAT * COLUMNS
UNITS = 64
HIDDEN = FEAT * UNITS
PAIRS = KINDS // 2
NODES = GROUPS * CAPACITY
WEIGHT_LANES = 256
MESSAGE = NODES + WEIGHT_LANES
Z = 16
CORES = 2
BLOCK = 2 * CORES
BLOCKS = Z * CORES // BLOCK
HALF = COLUMNS // CORES
FIRST_ROWS = PAIRS * HALF
SECOND_ROWS = 16
SHARD_ROWS = SECOND_ROWS + FIRST_ROWS
CLASS_ROWS = 160
SIDE = 4
ADJ_ROWS = RELATIONS * CAPACITY
ROWS = KINDS * TARGETS
GRAD_START = ADJ_ROWS + ROWS
DEGREE_START = GRAD_START + UNITS
DEGREE_ROWS = ROWS // 4
GRAPH_ROWS = DEGREE_START + DEGREE_ROWS
MIB = 1024 * 1024


def dot(a, b, contract):
    return lax.dot_general(a, b, ((contract[:1], contract[1:]), ((), ())), preferred_element_type=F32)


def eye(size):
    row = lax.broadcasted_iota(jnp.int32, (size, size), 0)
    column = lax.broadcasted_iota(jnp.int32, (size, size), 1)
    return (row == column).astype(F32).astype(BF16)


def swap_halves(tile):
    return pltpu.roll(tile, UNITS, 1)


def low_half(rows):
    return lax.broadcasted_iota(jnp.int32, (rows, 2 * UNITS), 1) < UNITS


def pack_kernel(core_ref, x_ref, w_ref, out_ref, x_tile, w_tiles, packed_ref, w_sem, x_sem, out_sem):
    load_x = pltpu.make_async_copy(x_ref, x_tile, w_sem.at[PAIRS])
    load_x.start()
    loads = []
    for pair in range(PAIRS):
        loads.append(pltpu.make_async_copy(w_ref.at[2 * pair + core_ref[0]], w_tiles.at[pair], w_sem.at[pair]))
        loads[-1].start()
    load_x.wait()
    stores = []
    for dest in range(FEAT):
        stores.append(pltpu.make_async_copy(x_tile, out_ref.at[dest, :, pl.ds(0, NODES)], x_sem.at[dest]))
        stores[-1].start()
    for load in loads:
        load.wait()
    low = low_half(COLUMNS)
    for tile in range(FEAT // 2):
        lanes = pl.ds(tile * 2 * UNITS, 2 * UNITS)
        first, second, third = [w_tiles[pair, :, lanes].astype(F32) for pair in range(PAIRS)]
        front = pl.ds(0, 2 * UNITS)
        back = pl.ds(2 * UNITS, 2 * UNITS)
        packed_ref[2 * tile, :, front] = jnp.where(low, first, swap_halves(second)).astype(BF16)
        packed_ref[2 * tile, :, back] = third.astype(BF16)
        packed_ref[2 * tile + 1, :, front] = jnp.where(low, swap_halves(first), second).astype(BF16)
        packed_ref[2 * tile + 1, :, back] = swap_halves(third).astype(BF16)
    stores.append(pltpu.make_async_copy(packed_ref, out_ref.at[:, :, pl.ds(NODES, WEIGHT_LANES)], out_sem))
    stores[-1].start()
    for store in stores:
        store.wait()


def live_slots(ids, count):
    node = lax.broadcasted_iota(jnp.int32, (SLOTS, CAPACITY), 1)
    return (ids >= 0) & (ids < count) & (node < count)


def adjacency_kernel(
    counts_ref,
    offsets_ref,
    slots_ref,
    weight_ref,
    upstream_ref,
    adj_ref,
    value_ref,
):
    tile_row = lax.broadcasted_iota(jnp.int32, (16, CAPACITY), 0).astype(F32).astype(BF16)
    one = jnp.ones((16, CAPACITY), BF16)
    zero = jnp.zeros((16, CAPACITY), BF16)
    target = lax.broadcasted_iota(jnp.int32, (TARGETS, CAPACITY), 0)
    place = lax.broadcasted_iota(jnp.int32, (TARGETS, CAPACITY), 1)
    half = CAPACITY // 2
    for group in range(GROUPS):
        count = counts_ref[group]
        pick = (place == target + offsets_ref[group]).astype(F32).astype(BF16)
        adj_ref[group, ADJ_ROWS : ADJ_ROWS + TARGETS, :] = pick

        def relation_step(relation, carry, group=group, count=count, pick=pick):
            ids = slots_ref[group, relation]
            live = live_slots(ids, count)
            origin = pl.multiple_of(relation * CAPACITY, CAPACITY)
            for part in range(2):
                inside = live & (ids >= part * half) & (ids < (part + 1) * half)
                value = jnp.where(inside, ids - part * half, -1).astype(F32)
                for slot in range(SLOTS):
                    value_ref[part, slot] = jnp.broadcast_to(
                        value[slot : slot + 1, :], (16, CAPACITY)
                    ).astype(BF16)
            for part in range(2):

                def tile_step(step, carry, part=part):
                    base = step * 32
                    here = tile_row + base.astype(F32).astype(BF16)
                    there = here + jnp.full((), 16, BF16)
                    first = zero
                    second = zero
                    for slot in range(SLOTS):
                        value = value_ref[part, slot]
                        first = first + jnp.where(value == here, one, zero)
                        second = second + jnp.where(value == there, one, zero)
                    start = pl.multiple_of(origin + part * half + base, 32)
                    adj_ref[group, pl.ds(start, 16), :] = first
                    adj_ref[group, pl.ds(start + 16, 16), :] = second
                    return carry

                lax.fori_loop(0, half // 32, tile_step, 0)
            start = pl.multiple_of(ADJ_ROWS + (relation + 1) * TARGETS, TARGETS)
            adj_ref[group, pl.ds(start, TARGETS), :] = dot(
                pick, adj_ref[group, pl.ds(origin, CAPACITY), :], (1, 1)
            ).astype(BF16)
            return carry

        lax.fori_loop(0, RELATIONS, relation_step, 0)
        rows = adj_ref[group, ADJ_ROWS:GRAD_START, :]
        degree = jnp.maximum(jnp.sum(rows.astype(F32), axis=1, keepdims=True), 1.0)
        for part in range(4):
            piece = degree[part * DEGREE_ROWS : (part + 1) * DEGREE_ROWS]
            adj_ref[group, DEGREE_START:, part * 2 * UNITS : (part + 1) * 2 * UNITS] = jnp.broadcast_to(
                piece, (DEGREE_ROWS, 2 * UNITS)
            ).astype(BF16)
        upstream = upstream_ref[group * TARGETS : (group + 1) * TARGETS, :]
        returned = []
        for kind in range(KINDS):
            returned.append(dot(upstream, weight_ref[kind * UNITS : (kind + 1) * UNITS, :], (1, 1)))
        spread = (jnp.concatenate(returned, axis=0) / degree).astype(BF16)
        adj_ref[group, GRAD_START:DEGREE_START, :] = dot(spread, rows, (0, 0)).astype(BF16)


def layer_kernel(
    core_ref,
    counts_ref,
    message_ref,
    first_ref,
    slots_ref,
    bias_ref,
    weight_ref,
    upstream_ref,
    adj_from,
    keep_ref,
    send_ref,
    score_ref,
    adj_ref,
    adj_sem,
    mixed_ref,
    low_ref,
    high_ref,
    whole_ref,
):
    def fetch(group, relation):
        size = CAPACITY if relation < RELATIONS else GRAPH_ROWS - ADJ_ROWS
        rows = pl.ds(relation * CAPACITY, size)
        return pltpu.make_async_copy(
            adj_from.at[group, rows], adj_ref.at[group, rows], adj_sem.at[group, relation]
        )

    for group in range(GROUPS):
        for relation in range(KINDS):
            fetch(group, relation).start()
    turn = eye(WEIGHT_LANES)
    first_weight = [dot(turn, first_ref[part], (1, 1)).astype(BF16) for part in range(CORES)]
    size = WIDTH // 3
    preacts = []
    for group in range(GROUPS):
        lanes = slice(group * CAPACITY, (group + 1) * CAPACITY)
        count = counts_ref[group]
        for relation in range(RELATIONS):
            fetch(group, relation).wait()
            adjacency = adj_ref[group, relation * CAPACITY : (relation + 1) * CAPACITY, :]
            live = live_slots(slots_ref[group, relation], count)
            inverse = 1.0 / jnp.maximum(jnp.sum(live.astype(F32), axis=0, keepdims=True), 1.0)
            for block in range(3):
                mixed = dot(message_ref[block * size : (block + 1) * size, lanes], adjacency, (1, 0))
                start = relation * WIDTH + block * size
                mixed_ref[group, start : start + size, :] = (mixed * inverse).astype(BF16)
        preact = bias_ref[...] + dot(first_weight[0][:UNITS], message_ref[:, lanes], (1, 0))
        for kind in range(1, KINDS):
            preact = preact + dot(
                first_weight[kind % CORES][kind // CORES * UNITS : (kind // CORES + 1) * UNITS],
                mixed_ref[group, (kind - 1) * WIDTH : kind * WIDTH, :],
                (1, 0),
            )
        preacts.append(preact)
    hiddens = []
    for group, preact in enumerate(preacts):
        fetch(group, RELATIONS).wait()
        hiddens.append(jnp.maximum(preact, 0.0).astype(BF16))
        pre_grad = jnp.where(preact > 0, adj_ref[group, GRAD_START:DEGREE_START, :].astype(F32), 0.0)
        nothing = jnp.zeros_like(pre_grad)
        low_ref[group] = jnp.concatenate([pre_grad, nothing], axis=0).astype(BF16)
        high_ref[group] = jnp.concatenate([nothing, pre_grad], axis=0).astype(BF16)
    score_parts = []
    grad_second = jnp.zeros((CLASSES, KINDS * UNITS), F32)
    for group, hidden in enumerate(hiddens):
        rows = adj_ref[group, ADJ_ROWS:GRAD_START, :]
        degree = adj_ref[group, DEGREE_START:, :].astype(F32)
        degree = jnp.concatenate([degree[:, part * 2 * UNITS : part * 2 * UNITS + UNITS] for part in range(4)], axis=0)
        second_in = dot(rows, hidden, (1, 1)) / degree
        wide = jnp.concatenate(
            [second_in[kind * TARGETS : (kind + 1) * TARGETS] for kind in range(KINDS)], axis=1
        ).astype(BF16)
        score_parts.append(dot(weight_ref[...], wide, (0, 1)))
        upstream = upstream_ref[group * TARGETS : (group + 1) * TARGETS, :]
        grad_second = grad_second + dot(upstream, wide, (0, 0))
    tail = jnp.zeros((CLASS_ROWS - CLASSES, 2 * UNITS), F32)
    score = jnp.concatenate([jnp.concatenate(score_parts, axis=1), tail], axis=0)
    score_ref[...] = score
    for pair in range(PAIRS):
        total = jnp.zeros((WIDTH, 2 * UNITS), F32)
        for group in range(GROUPS):
            lanes = slice(group * CAPACITY, (group + 1) * CAPACITY)
            if pair == 0:
                even = message_ref[:, lanes]
            else:
                even = mixed_ref[group, (2 * pair - 1) * WIDTH : 2 * pair * WIDTH, :]
            odd = mixed_ref[group, 2 * pair * WIDTH : (2 * pair + 1) * WIDTH, :]
            total = total + dot(even, low_ref[group], (1, 1)) + dot(odd, high_ref[group], (1, 1))
        total = total.reshape(FEAT, COLUMNS, 2 * UNITS)
        start = SECOND_ROWS + pair * HALF
        for part in range(CORES):
            whole_ref[part, :, start : start + HALF, :] = total[:, part * HALF : (part + 1) * HALF, :]
    packed = []
    for pair in range(PAIRS):
        packed.append(grad_second[:, pair * 2 * UNITS : (pair + 1) * 2 * UNITS])
        packed.append(tail)
    packed.append(jnp.zeros((Z * CORES * SECOND_ROWS - PAIRS * CLASS_ROWS, 2 * UNITS), F32))
    packed = jnp.concatenate(packed, axis=0).reshape(Z, CORES, SECOND_ROWS, 2 * UNITS)
    for part in range(CORES):
        whole_ref[part, :, :SECOND_ROWS, :] = packed[:, part]
    core = core_ref[0]
    keep_ref[...] = whole_ref[core]
    send_ref[...] = whole_ref[1 - core].astype(BF16)


def merge_kernel(core_ref, keep_ref, both_ref, message_ref, second_ref):
    chip = keep_ref[...] + both_ref[1 - core_ref[0]].astype(F32)
    message_ref[...] = chip[:, SECOND_ROWS:, :].astype(BF16)
    second_ref[...] = chip[:, :SECOND_ROWS, :].astype(BF16)


def relay_kernel(message_ref, second_ref, score_ref, shards_ref, passed_ref):
    shards_ref[:, SECOND_ROWS:, :] = message_ref[...]
    shards_ref[:, :SECOND_ROWS, :] = second_ref[...]
    passed_ref[...] = score_ref[...]


def fold_kernel(pieces_ref, s0_ref, s1_ref, s2_ref, s3_ref, copies_ref, score_ref):
    total = pieces_ref[0].astype(F32)
    for part in range(1, Z):
        total = total + pieces_ref[part].astype(F32)
    total = total.astype(BF16)
    for part in range(BLOCKS):
        copies_ref[part] = total
    score_ref[...] = s0_ref[...] + s1_ref[...] + s2_ref[...] + s3_ref[...]


def unpack_kernel(shards_ref, s0_ref, s1_ref, s2_ref, s3_ref, first_ref, second_ref, logits_ref):
    low = low_half(HALF)
    for tile in range(FEAT // 2):
        lanes = pl.ds(tile * 2 * UNITS, 2 * UNITS)
        for part in range(CORES):
            left = shards_ref[part, tile].astype(F32)
            right = shards_ref[CORES + part, tile].astype(F32)
            rows = pl.ds(part * HALF, HALF)
            for pair in range(PAIRS):
                start = SECOND_ROWS + pair * HALF
                a = left[start : start + HALF]
                b = right[start : start + HALF]
                first_ref[2 * pair, rows, lanes] = jnp.where(low, a, swap_halves(b))
                first_ref[2 * pair + 1, rows, lanes] = jnp.where(low, swap_halves(a), b)
    packed = jnp.stack([shards_ref[part, :, :SECOND_ROWS, :] for part in range(BLOCK)], axis=1)
    packed = packed.reshape(Z * CORES * SECOND_ROWS, 2 * UNITS)
    identity = eye(2 * UNITS)
    for pair in range(PAIRS):
        block = packed[pair * CLASS_ROWS : (pair + 1) * CLASS_ROWS]
        turned = dot(identity, block, (1, 1))
        second_ref[2 * pair] = turned[:UNITS, :CLASSES]
        second_ref[2 * pair + 1] = turned[UNITS:, :CLASSES]
    logits_ref[...] = (s0_ref[...] + s1_ref[...] + s2_ref[...] + s3_ref[...])[:CLASSES]


VMEM = pl.BlockSpec(memory_space=pltpu.VMEM)
SMEM = pl.BlockSpec(memory_space=pltpu.SMEM)


def params(mib):
    return pltpu.CompilerParams(vmem_limit_bytes=mib * MIB)


def cost(flops, size):
    return pl.CostEstimate(flops=flops, bytes_accessed=size, transcendentals=0)


def shape(*dims, dtype=BF16):
    return jax.ShapeDtypeStruct(dims, dtype)


def pack(core, x, w):
    anywhere = pl.BlockSpec(memory_space=pl.ANY)
    return pl.pallas_call(
        pack_kernel,
        out_shape=shape(FEAT, COLUMNS, MESSAGE),
        in_specs=[SMEM, anywhere, anywhere],
        out_specs=anywhere,
        scratch_shapes=[
            pltpu.VMEM((COLUMNS, NODES), BF16),
            pltpu.VMEM((PAIRS, COLUMNS, HIDDEN), BF16),
            pltpu.VMEM((FEAT, COLUMNS, WEIGHT_LANES), BF16),
            pltpu.SemaphoreType.DMA((PAIRS + 1,)),
            pltpu.SemaphoreType.DMA((FEAT,)),
            pltpu.SemaphoreType.DMA,
        ],
        compiler_params=params(58),
    )(core, x, w)


def adjacency(counts, offsets, slots, weight, upstream):
    return pl.pallas_call(
        adjacency_kernel,
        out_shape=shape(GROUPS, GRAPH_ROWS, CAPACITY),
        in_specs=[SMEM] * 2 + [VMEM] * 3,
        out_specs=VMEM,
        scratch_shapes=[pltpu.VMEM((2, SLOTS, 16, CAPACITY), BF16)],
        compiler_params=params(58),
        cost_estimate=cost(8 * 10**9, 8 * MIB),
    )(counts, offsets, slots, weight, upstream)


def layers(core, counts, message, first, slots, bias, weight, upstream, adj):
    shard = shape(Z, SHARD_ROWS, 2 * UNITS, dtype=F32)
    return pl.pallas_call(
        layer_kernel,
        out_shape=(shard, shape(Z, SHARD_ROWS, 2 * UNITS), shape(CLASS_ROWS, GROUPS * TARGETS, dtype=F32)),
        in_specs=[SMEM] * 2 + [VMEM] * 6 + [pl.BlockSpec(memory_space=pl.ANY)],
        out_specs=(VMEM, VMEM, VMEM),
        scratch_shapes=[
            pltpu.VMEM(adj.shape, BF16),
            pltpu.SemaphoreType.DMA((GROUPS, KINDS)),
            pltpu.VMEM((GROUPS, RELATIONS * WIDTH, CAPACITY), BF16),
            pltpu.VMEM((GROUPS, 2 * UNITS, CAPACITY), BF16),
            pltpu.VMEM((GROUPS, 2 * UNITS, CAPACITY), BF16),
            pltpu.VMEM((CORES, Z, SHARD_ROWS, 2 * UNITS), F32),
        ],
        compiler_params=params(44),
        cost_estimate=cost(12 * 10**9, 12 * MIB),
    )(core, counts, message, first, slots, bias, weight, upstream, adj)


def merge(core, keep, both):
    return pl.pallas_call(
        merge_kernel,
        out_shape=(shape(FEAT, FIRST_ROWS, 2 * UNITS), shape(Z, SECOND_ROWS, 2 * UNITS)),
        in_specs=[SMEM] + [VMEM] * 2,
        out_specs=(VMEM,) * 2,
        compiler_params=params(8),
    )(core, keep, both)


def relay(message, second, score):
    return pl.pallas_call(
        relay_kernel,
        out_shape=(shape(Z, SHARD_ROWS, 2 * UNITS), shape(*score.shape, dtype=F32)),
        in_specs=[VMEM] * 3,
        out_specs=(VMEM,) * 2,
        compiler_params=params(8),
    )(message, second, score)


def fold(pieces, scores):
    return pl.pallas_call(
        fold_kernel,
        out_shape=(shape(BLOCKS, SHARD_ROWS, 2 * UNITS), shape(*scores[0].shape, dtype=F32)),
        in_specs=[VMEM] * 5,
        out_specs=(VMEM,) * 2,
        compiler_params=params(8),
    )(pieces, *scores)


def row_hops(step):
    return [(i, i // SIDE * SIDE + (i + step) % SIDE) for i in range(FEAT)]


def column_hops(step):
    return [(i, (i + step * SIDE) % FEAT) for i in range(FEAT)]


def spread_out(score, hops):
    return [score] + [lax.ppermute(score, "feat", hops(step)) for step in range(1, SIDE)]


def unpack(shards, scores):
    return pl.pallas_call(
        unpack_kernel,
        out_shape=(
            shape(KINDS, COLUMNS, HIDDEN, dtype=F32),
            shape(KINDS, UNITS, CLASSES, dtype=F32),
            shape(CLASSES, GROUPS * TARGETS, dtype=F32),
        ),
        in_specs=[VMEM] * 5,
        out_specs=(VMEM, VMEM, VMEM),
        compiler_params=params(8),
    )(shards, *scores)


def local(
    vertex_embeddings,
    adjacent_vertices,
    node_counts,
    target_offsets,
    weight_one,
    bias_one,
    weight_two,
    score_derivative,
):
    core = (lax.axis_index("batch") % CORES).astype(jnp.int32).reshape(1)
    chips = [[z * CORES + c for c in range(CORES)] for z in range(Z)]
    same_core = [[z * CORES + c for z in range(Z)] for c in range(CORES)]
    message = lax.all_to_all(pack(core, vertex_embeddings.T, weight_one), "feat", 0, 0)
    message = message.reshape(WIDTH, MESSAGE)
    first = lax.all_gather(message[:, NODES:], "batch", axis_index_groups=chips)
    slots = jnp.swapaxes(adjacent_vertices, 2, 3)
    weight = weight_two.reshape(KINDS * UNITS, CLASSES)
    adj = adjacency(node_counts, target_offsets, slots, weight, score_derivative)
    keep, send, score = layers(
        core,
        node_counts,
        message,
        first,
        slots,
        bias_one.reshape(UNITS, 1),
        weight,
        score_derivative,
        adj,
    )
    both = lax.all_gather(send, "batch", axis_index_groups=chips)
    message, second = merge(core, keep, both)
    message = lax.all_to_all(message, "feat", 0, 0)
    shards, score = relay(message, second, score)
    pieces = lax.all_to_all(shards, "batch", 0, 0, axis_index_groups=same_core)
    copies, score = fold(pieces, spread_out(score, row_hops))
    blocks = [[block * BLOCK + i for i in range(BLOCK)] for block in range(BLOCKS)]
    same_place = [[block * BLOCK + i for block in range(BLOCKS)] for i in range(BLOCK)]
    shards = lax.all_to_all(copies, "batch", 0, 0, axis_index_groups=same_place)
    scores = spread_out(score, column_hops)
    shards = lax.all_gather(shards, "batch", axis_index_groups=blocks)
    first_grad, second_grad, logits = unpack(shards, scores)
    return (logits.T, first_grad, second_grad)


def solution(mesh):
    placed = (
        P("batch", "feat"),
        P("batch", None, None, None),
        P("batch"),
        P("batch"),
        P(None, "feat", None),
        P("feat"),
        P(None, "feat", None),
        P("batch", None),
    )
    return jax.shard_map(
        local,
        mesh=mesh,
        in_specs=placed,
        out_specs=(P("batch", None), P(None, "feat", None), P(None, "feat", None)),
        check_vma=False,
    )
```

```python
import jax
import jax.numpy as jnp
from jax import lax
from jax.experimental import pallas as pl
from jax.experimental.pallas import tpu as pltpu
from jax.sharding import PartitionSpec as P

BF16 = jnp.bfloat16
F32 = jnp.float32

GROUPS = 2
CAPACITY = 512
RELATIONS = 5
KINDS = RELATIONS + 1
SLOTS = 8
TARGETS = 64
CLASSES = 153
FEAT = 16
COLUMNS = 48
WIDTH = FEAT * COLUMNS
UNITS = 64
HIDDEN = FEAT * UNITS
PAIRS = KINDS // 2
NODES = GROUPS * CAPACITY
WEIGHT_LANES = 256
MESSAGE = NODES + WEIGHT_LANES
Z = 16
CORES = 2
BLOCK = 2 * CORES
BLOCKS = Z * CORES // BLOCK
HALF = COLUMNS // CORES
FIRST_ROWS = PAIRS * HALF
SECOND_ROWS = 16
SHARD_ROWS = SECOND_ROWS + FIRST_ROWS
CLASS_ROWS = 160
SIDE = 4
ADJ_ROWS = RELATIONS * CAPACITY
ROWS = KINDS * TARGETS
GRAD_START = ADJ_ROWS + ROWS
DEGREE_START = GRAD_START + UNITS
DEGREE_ROWS = ROWS // 4
GRAPH_ROWS = DEGREE_START + DEGREE_ROWS
MIB = 1024 * 1024


def dot(a, b, contract):
    return lax.dot_general(a, b, ((contract[:1], contract[1:]), ((), ())), preferred_element_type=F32)


def eye(size):
    row = lax.broadcasted_iota(jnp.int32, (size, size), 0)
    column = lax.broadcasted_iota(jnp.int32, (size, size), 1)
    return (row == column).astype(F32).astype(BF16)


def swap_halves(tile):
    return pltpu.roll(tile, UNITS, 1)


def low_half(rows):
    return lax.broadcasted_iota(jnp.int32, (rows, 2 * UNITS), 1) < UNITS


def pack_kernel(core_ref, x_ref, w_ref, out_ref, x_tile, w_tiles, packed_ref, w_sem, x_sem, out_sem):
    load_x = pltpu.make_async_copy(x_ref, x_tile, w_sem.at[PAIRS])
    load_x.start()
    loads = []
    for pair in range(PAIRS):
        loads.append(pltpu.make_async_copy(w_ref.at[2 * pair + core_ref[0]], w_tiles.at[pair], w_sem.at[pair]))
        loads[-1].start()
    load_x.wait()
    stores = []
    for dest in range(FEAT):
        stores.append(pltpu.make_async_copy(x_tile, out_ref.at[dest, :, pl.ds(0, NODES)], x_sem.at[dest]))
        stores[-1].start()
    for load in loads:
        load.wait()
    low = low_half(COLUMNS)
    for tile in range(FEAT // 2):
        lanes = pl.ds(tile * 2 * UNITS, 2 * UNITS)
        first, second, third = [w_tiles[pair, :, lanes].astype(F32) for pair in range(PAIRS)]
        front = pl.ds(0, 2 * UNITS)
        back = pl.ds(2 * UNITS, 2 * UNITS)
        packed_ref[2 * tile, :, front] = jnp.where(low, first, swap_halves(second)).astype(BF16)
        packed_ref[2 * tile, :, back] = third.astype(BF16)
        packed_ref[2 * tile + 1, :, front] = jnp.where(low, swap_halves(first), second).astype(BF16)
        packed_ref[2 * tile + 1, :, back] = swap_halves(third).astype(BF16)
    stores.append(pltpu.make_async_copy(packed_ref, out_ref.at[:, :, pl.ds(NODES, WEIGHT_LANES)], out_sem))
    stores[-1].start()
    for store in stores:
        store.wait()


def live_slots(ids, count):
    node = lax.broadcasted_iota(jnp.int32, (SLOTS, CAPACITY), 1)
    return (ids >= 0) & (ids < count) & (node < count)


def adjacency_kernel(
    counts_ref,
    offsets_ref,
    slots_ref,
    weight_ref,
    upstream_ref,
    adj_ref,
    value_ref,
):
    tile_row = lax.broadcasted_iota(jnp.int32, (16, CAPACITY), 0).astype(F32).astype(BF16)
    one = jnp.ones((16, CAPACITY), BF16)
    zero = jnp.zeros((16, CAPACITY), BF16)
    target = lax.broadcasted_iota(jnp.int32, (TARGETS, CAPACITY), 0)
    place = lax.broadcasted_iota(jnp.int32, (TARGETS, CAPACITY), 1)
    half = CAPACITY // 2
    for group in range(GROUPS):
        count = counts_ref[group]
        pick = (place == target + offsets_ref[group]).astype(F32).astype(BF16)
        adj_ref[group, ADJ_ROWS : ADJ_ROWS + TARGETS, :] = pick

        def relation_step(relation, carry, group=group, count=count, pick=pick):
            ids = slots_ref[group, relation]
            live = live_slots(ids, count)
            origin = pl.multiple_of(relation * CAPACITY, CAPACITY)
            for part in range(2):
                inside = live & (ids >= part * half) & (ids < (part + 1) * half)
                value = jnp.where(inside, ids - part * half, -1).astype(F32)
                for slot in range(SLOTS):
                    value_ref[part, slot] = jnp.broadcast_to(
                        value[slot : slot + 1, :], (16, CAPACITY)
                    ).astype(BF16)
            for part in range(2):

                def tile_step(step, carry, part=part):
                    base = step * 32
                    here = tile_row + base.astype(F32).astype(BF16)
                    there = here + jnp.full((), 16, BF16)
                    first = zero
                    second = zero
                    for slot in range(SLOTS):
                        value = value_ref[part, slot]
                        first = first + jnp.where(value == here, one, zero)
                        second = second + jnp.where(value == there, one, zero)
                    start = pl.multiple_of(origin + part * half + base, 32)
                    adj_ref[group, pl.ds(start, 16), :] = first
                    adj_ref[group, pl.ds(start + 16, 16), :] = second
                    return carry

                lax.fori_loop(0, half // 32, tile_step, 0)
            start = pl.multiple_of(ADJ_ROWS + (relation + 1) * TARGETS, TARGETS)
            adj_ref[group, pl.ds(start, TARGETS), :] = dot(
                pick, adj_ref[group, pl.ds(origin, CAPACITY), :], (1, 1)
            ).astype(BF16)
            return carry

        lax.fori_loop(0, RELATIONS, relation_step, 0)
        rows = adj_ref[group, ADJ_ROWS:GRAD_START, :]
        degree = jnp.maximum(jnp.sum(rows.astype(F32), axis=1, keepdims=True), 1.0)
        for part in range(4):
            piece = degree[part * DEGREE_ROWS : (part + 1) * DEGREE_ROWS]
            adj_ref[group, DEGREE_START:, part * 2 * UNITS : (part + 1) * 2 * UNITS] = jnp.broadcast_to(
                piece, (DEGREE_ROWS, 2 * UNITS)
            ).astype(BF16)
        upstream = upstream_ref[group * TARGETS : (group + 1) * TARGETS, :]
        returned = []
        for kind in range(KINDS):
            returned.append(dot(upstream, weight_ref[kind * UNITS : (kind + 1) * UNITS, :], (1, 1)))
        spread = (jnp.concatenate(returned, axis=0) / degree).astype(BF16)
        adj_ref[group, GRAD_START:DEGREE_START, :] = dot(spread, rows, (0, 0)).astype(BF16)


def layer_kernel(
    core_ref,
    counts_ref,
    message_ref,
    first_ref,
    slots_ref,
    bias_ref,
    weight_ref,
    upstream_ref,
    adj_from,
    keep_ref,
    send_ref,
    score_ref,
    adj_ref,
    adj_sem,
    mixed_ref,
    low_ref,
    high_ref,
    whole_ref,
):
    def fetch(group, relation):
        size = CAPACITY if relation < RELATIONS else GRAPH_ROWS - ADJ_ROWS
        rows = pl.ds(relation * CAPACITY, size)
        return pltpu.make_async_copy(
            adj_from.at[group, rows], adj_ref.at[group, rows], adj_sem.at[group, relation]
        )

    for group in range(GROUPS):
        for relation in range(KINDS):
            fetch(group, relation).start()
    turn = eye(WEIGHT_LANES)
    first_weight = [dot(turn, first_ref[part], (1, 1)).astype(BF16) for part in range(CORES)]
    size = WIDTH // 3
    preacts = []
    for group in range(GROUPS):
        lanes = slice(group * CAPACITY, (group + 1) * CAPACITY)
        count = counts_ref[group]
        for relation in range(RELATIONS):
            fetch(group, relation).wait()
            adjacency = adj_ref[group, relation * CAPACITY : (relation + 1) * CAPACITY, :]
            live = live_slots(slots_ref[group, relation], count)
            inverse = 1.0 / jnp.maximum(jnp.sum(live.astype(F32), axis=0, keepdims=True), 1.0)
            for block in range(3):
                mixed = dot(message_ref[block * size : (block + 1) * size, lanes], adjacency, (1, 0))
                start = relation * WIDTH + block * size
                mixed_ref[group, start : start + size, :] = (mixed * inverse).astype(BF16)
        preact = bias_ref[...] + dot(first_weight[0][:UNITS], message_ref[:, lanes], (1, 0))
        for kind in range(1, KINDS):
            preact = preact + dot(
                first_weight[kind % CORES][kind // CORES * UNITS : (kind // CORES + 1) * UNITS],
                mixed_ref[group, (kind - 1) * WIDTH : kind * WIDTH, :],
                (1, 0),
            )
        preacts.append(preact)
    hiddens = []
    for group, preact in enumerate(preacts):
        fetch(group, RELATIONS).wait()
        hiddens.append(jnp.maximum(preact, 0.0).astype(BF16))
        pre_grad = jnp.where(preact > 0, adj_ref[group, GRAD_START:DEGREE_START, :].astype(F32), 0.0)
        nothing = jnp.zeros_like(pre_grad)
        low_ref[group] = jnp.concatenate([pre_grad, nothing], axis=0).astype(BF16)
        high_ref[group] = jnp.concatenate([nothing, pre_grad], axis=0).astype(BF16)
    score_parts = []
    grad_second = jnp.zeros((CLASSES, KINDS * UNITS), F32)
    for group, hidden in enumerate(hiddens):
        rows = adj_ref[group, ADJ_ROWS:GRAD_START, :]
        degree = adj_ref[group, DEGREE_START:, :].astype(F32)
        degree = jnp.concatenate([degree[:, part * 2 * UNITS : part * 2 * UNITS + UNITS] for part in range(4)], axis=0)
        second_in = dot(rows, hidden, (1, 1)) / degree
        wide = jnp.concatenate(
            [second_in[kind * TARGETS : (kind + 1) * TARGETS] for kind in range(KINDS)], axis=1
        ).astype(BF16)
        score_parts.append(dot(weight_ref[...], wide, (0, 1)))
        upstream = upstream_ref[group * TARGETS : (group + 1) * TARGETS, :]
        grad_second = grad_second + dot(upstream, wide, (0, 0))
    tail = jnp.zeros((CLASS_ROWS - CLASSES, 2 * UNITS), F32)
    score = jnp.concatenate([jnp.concatenate(score_parts, axis=1), tail], axis=0)
    score_ref[...] = score
    for pair in range(PAIRS):
        total = jnp.zeros((WIDTH, 2 * UNITS), F32)
        for group in range(GROUPS):
            lanes = slice(group * CAPACITY, (group + 1) * CAPACITY)
            if pair == 0:
                even = message_ref[:, lanes]
            else:
                even = mixed_ref[group, (2 * pair - 1) * WIDTH : 2 * pair * WIDTH, :]
            odd = mixed_ref[group, 2 * pair * WIDTH : (2 * pair + 1) * WIDTH, :]
            total = total + dot(even, low_ref[group], (1, 1)) + dot(odd, high_ref[group], (1, 1))
        total = total.reshape(FEAT, COLUMNS, 2 * UNITS)
        start = SECOND_ROWS + pair * HALF
        for part in range(CORES):
            whole_ref[part, :, start : start + HALF, :] = total[:, part * HALF : (part + 1) * HALF, :]
    packed = []
    for pair in range(PAIRS):
        packed.append(grad_second[:, pair * 2 * UNITS : (pair + 1) * 2 * UNITS])
        packed.append(tail)
    packed.append(jnp.zeros((Z * CORES * SECOND_ROWS - PAIRS * CLASS_ROWS, 2 * UNITS), F32))
    packed = jnp.concatenate(packed, axis=0).reshape(Z, CORES, SECOND_ROWS, 2 * UNITS)
    for part in range(CORES):
        whole_ref[part, :, :SECOND_ROWS, :] = packed[:, part]
    core = core_ref[0]
    keep_ref[...] = whole_ref[core]
    send_ref[...] = whole_ref[1 - core].astype(BF16)


def merge_kernel(core_ref, keep_ref, both_ref, message_ref, second_ref):
    chip = keep_ref[...] + both_ref[1 - core_ref[0]].astype(F32)
    message_ref[...] = chip[:, SECOND_ROWS:, :].astype(BF16)
    second_ref[...] = chip[:, :SECOND_ROWS, :].astype(BF16)


def relay_kernel(message_ref, second_ref, score_ref, shards_ref, passed_ref):
    shards_ref[:, SECOND_ROWS:, :] = message_ref[...]
    shards_ref[:, :SECOND_ROWS, :] = second_ref[...]
    passed_ref[...] = score_ref[...]


def fold_kernel(pieces_ref, s0_ref, s1_ref, s2_ref, s3_ref, copies_ref, score_ref):
    total = pieces_ref[0].astype(F32)
    for part in range(1, Z):
        total = total + pieces_ref[part].astype(F32)
    total = total.astype(BF16)
    for part in range(BLOCKS):
        copies_ref[part] = total
    score_ref[...] = s0_ref[...] + s1_ref[...] + s2_ref[...] + s3_ref[...]


def unpack_kernel(
    shards_ref,
    s0_ref,
    s1_ref,
    s2_ref,
    s3_ref,
    first_to,
    second_to,
    logits_ref,
    first_ref,
    second_ref,
    first_sem,
    second_sem,
):
    low = low_half(HALF)
    stores = []
    for pair in range(PAIRS):
        for tile in range(FEAT // 2):
            lanes = pl.ds(tile * 2 * UNITS, 2 * UNITS)
            for part in range(CORES):
                left = shards_ref[part, tile].astype(F32)
                right = shards_ref[CORES + part, tile].astype(F32)
                rows = pl.ds(part * HALF, HALF)
                start = SECOND_ROWS + pair * HALF
                a = left[start : start + HALF]
                b = right[start : start + HALF]
                first_ref[2 * pair, rows, lanes] = jnp.where(low, a, swap_halves(b))
                first_ref[2 * pair + 1, rows, lanes] = jnp.where(low, swap_halves(a), b)
        both = pl.ds(2 * pair, 2)
        stores.append(pltpu.make_async_copy(first_ref.at[both], first_to.at[both], first_sem.at[pair]))
        stores[-1].start()
    packed = jnp.stack([shards_ref[part, :, :SECOND_ROWS, :] for part in range(BLOCK)], axis=1)
    packed = packed.reshape(Z * CORES * SECOND_ROWS, 2 * UNITS)
    identity = eye(2 * UNITS)
    for pair in range(PAIRS):
        block = packed[pair * CLASS_ROWS : (pair + 1) * CLASS_ROWS]
        turned = dot(identity, block, (1, 1))
        second_ref[2 * pair] = turned[:UNITS, :CLASSES]
        second_ref[2 * pair + 1] = turned[UNITS:, :CLASSES]
    stores.append(pltpu.make_async_copy(second_ref, second_to, second_sem))
    stores[-1].start()
    logits_ref[...] = (s0_ref[...] + s1_ref[...] + s2_ref[...] + s3_ref[...])[:CLASSES]
    for store in stores:
        store.wait()


VMEM = pl.BlockSpec(memory_space=pltpu.VMEM)
SMEM = pl.BlockSpec(memory_space=pltpu.SMEM)


def params(mib):
    return pltpu.CompilerParams(vmem_limit_bytes=mib * MIB)


def cost(flops, size):
    return pl.CostEstimate(flops=flops, bytes_accessed=size, transcendentals=0)


def shape(*dims, dtype=BF16):
    return jax.ShapeDtypeStruct(dims, dtype)


def pack(core, x, w):
    anywhere = pl.BlockSpec(memory_space=pl.ANY)
    return pl.pallas_call(
        pack_kernel,
        out_shape=shape(FEAT, COLUMNS, MESSAGE),
        in_specs=[SMEM, anywhere, anywhere],
        out_specs=anywhere,
        scratch_shapes=[
            pltpu.VMEM((COLUMNS, NODES), BF16),
            pltpu.VMEM((PAIRS, COLUMNS, HIDDEN), BF16),
            pltpu.VMEM((FEAT, COLUMNS, WEIGHT_LANES), BF16),
            pltpu.SemaphoreType.DMA((PAIRS + 1,)),
            pltpu.SemaphoreType.DMA((FEAT,)),
            pltpu.SemaphoreType.DMA,
        ],
        compiler_params=params(58),
    )(core, x, w)


def adjacency(counts, offsets, slots, weight, upstream):
    return pl.pallas_call(
        adjacency_kernel,
        out_shape=shape(GROUPS, GRAPH_ROWS, CAPACITY),
        in_specs=[SMEM] * 2 + [VMEM] * 3,
        out_specs=VMEM,
        scratch_shapes=[pltpu.VMEM((2, SLOTS, 16, CAPACITY), BF16)],
        compiler_params=params(58),
        cost_estimate=cost(8 * 10**9, 8 * MIB),
    )(counts, offsets, slots, weight, upstream)


def layers(core, counts, message, first, slots, bias, weight, upstream, adj):
    shard = shape(Z, SHARD_ROWS, 2 * UNITS, dtype=F32)
    return pl.pallas_call(
        layer_kernel,
        out_shape=(shard, shape(Z, SHARD_ROWS, 2 * UNITS), shape(CLASS_ROWS, GROUPS * TARGETS, dtype=F32)),
        in_specs=[SMEM] * 2 + [VMEM] * 6 + [pl.BlockSpec(memory_space=pl.ANY)],
        out_specs=(VMEM, VMEM, VMEM),
        scratch_shapes=[
            pltpu.VMEM(adj.shape, BF16),
            pltpu.SemaphoreType.DMA((GROUPS, KINDS)),
            pltpu.VMEM((GROUPS, RELATIONS * WIDTH, CAPACITY), BF16),
            pltpu.VMEM((GROUPS, 2 * UNITS, CAPACITY), BF16),
            pltpu.VMEM((GROUPS, 2 * UNITS, CAPACITY), BF16),
            pltpu.VMEM((CORES, Z, SHARD_ROWS, 2 * UNITS), F32),
        ],
        compiler_params=params(44),
        cost_estimate=cost(12 * 10**9, 12 * MIB),
    )(core, counts, message, first, slots, bias, weight, upstream, adj)


def merge(core, keep, both):
    return pl.pallas_call(
        merge_kernel,
        out_shape=(shape(FEAT, FIRST_ROWS, 2 * UNITS), shape(Z, SECOND_ROWS, 2 * UNITS)),
        in_specs=[SMEM] + [VMEM] * 2,
        out_specs=(VMEM,) * 2,
        compiler_params=params(8),
    )(core, keep, both)


def relay(message, second, score):
    return pl.pallas_call(
        relay_kernel,
        out_shape=(shape(Z, SHARD_ROWS, 2 * UNITS), shape(*score.shape, dtype=F32)),
        in_specs=[VMEM] * 3,
        out_specs=(VMEM,) * 2,
        compiler_params=params(8),
    )(message, second, score)


def fold(pieces, scores):
    return pl.pallas_call(
        fold_kernel,
        out_shape=(shape(BLOCKS, SHARD_ROWS, 2 * UNITS), shape(*scores[0].shape, dtype=F32)),
        in_specs=[VMEM] * 5,
        out_specs=(VMEM,) * 2,
        compiler_params=params(8),
    )(pieces, *scores)


def row_hops(step):
    return [(i, i // SIDE * SIDE + (i + step) % SIDE) for i in range(FEAT)]


def column_hops(step):
    return [(i, (i + step * SIDE) % FEAT) for i in range(FEAT)]


def spread_out(score, hops):
    return [score] + [lax.ppermute(score, "feat", hops(step)) for step in range(1, SIDE)]


def unpack(shards, scores):
    return pl.pallas_call(
        unpack_kernel,
        out_shape=(
            shape(KINDS, COLUMNS, HIDDEN, dtype=F32),
            shape(KINDS, UNITS, CLASSES, dtype=F32),
            shape(CLASSES, GROUPS * TARGETS, dtype=F32),
        ),
        in_specs=[VMEM] * 5,
        out_specs=(pl.BlockSpec(memory_space=pl.ANY), pl.BlockSpec(memory_space=pl.ANY), VMEM),
        scratch_shapes=[
            pltpu.VMEM((KINDS, COLUMNS, HIDDEN), F32),
            pltpu.VMEM((KINDS, UNITS, CLASSES), F32),
            pltpu.SemaphoreType.DMA((PAIRS,)),
            pltpu.SemaphoreType.DMA,
        ],
        compiler_params=params(8),
    )(shards, *scores)


def local(
    vertex_embeddings,
    adjacent_vertices,
    node_counts,
    target_offsets,
    weight_one,
    bias_one,
    weight_two,
    score_derivative,
):
    core = (lax.axis_index("batch") % CORES).astype(jnp.int32).reshape(1)
    chips = [[z * CORES + c for c in range(CORES)] for z in range(Z)]
    same_core = [[z * CORES + c for z in range(Z)] for c in range(CORES)]
    message = lax.all_to_all(pack(core, vertex_embeddings.T, weight_one), "feat", 0, 0)
    message = message.reshape(WIDTH, MESSAGE)
    first = lax.all_gather(message[:, NODES:], "batch", axis_index_groups=chips)
    slots = jnp.swapaxes(adjacent_vertices, 2, 3)
    weight = weight_two.reshape(KINDS * UNITS, CLASSES)
    adj = adjacency(node_counts, target_offsets, slots, weight, score_derivative)
    keep, send, score = layers(
        core,
        node_counts,
        message,
        first,
        slots,
        bias_one.reshape(UNITS, 1),
        weight,
        score_derivative,
        adj,
    )
    both = lax.all_gather(send, "batch", axis_index_groups=chips)
    message, second = merge(core, keep, both)
    message = lax.all_to_all(message, "feat", 0, 0)
    shards, score = relay(message, second, score)
    pieces = lax.all_to_all(shards, "batch", 0, 0, axis_index_groups=same_core)
    copies, score = fold(pieces, spread_out(score, row_hops))
    blocks = [[block * BLOCK + i for i in range(BLOCK)] for block in range(BLOCKS)]
    same_place = [[block * BLOCK + i for block in range(BLOCKS)] for i in range(BLOCK)]
    shards = lax.all_to_all(copies, "batch", 0, 0, axis_index_groups=same_place)
    scores = spread_out(score, column_hops)
    shards = lax.all_gather(shards, "batch", axis_index_groups=blocks)
    first_grad, second_grad, logits = unpack(shards, scores)
    return (logits.T, first_grad, second_grad)


def solution(mesh):
    placed = (
        P("batch", "feat"),
        P("batch", None, None, None),
        P("batch"),
        P("batch"),
        P(None, "feat", None),
        P("feat"),
        P(None, "feat", None),
        P("batch", None),
    )
    return jax.shard_map(
        local,
        mesh=mesh,
        in_specs=placed,
        out_specs=(P("batch", None), P(None, "feat", None), P(None, "feat", None)),
        check_vma=False,
    )
```

```python
import jax
import jax.numpy as jnp
from jax import lax
from jax.experimental import pallas as pl
from jax.experimental.pallas import tpu as pltpu
from jax.sharding import PartitionSpec as P

BF16 = jnp.bfloat16
F32 = jnp.float32

GROUPS = 2
CAPACITY = 512
RELATIONS = 5
KINDS = RELATIONS + 1
SLOTS = 8
TARGETS = 64
CLASSES = 153
FEAT = 16
COLUMNS = 48
WIDTH = FEAT * COLUMNS
UNITS = 64
HIDDEN = FEAT * UNITS
PAIRS = KINDS // 2
NODES = GROUPS * CAPACITY
WEIGHT_LANES = 256
MESSAGE = NODES + WEIGHT_LANES
Z = 16
CORES = 2
BLOCK = 2 * CORES
BLOCKS = Z * CORES // BLOCK
HALF = COLUMNS // CORES
FIRST_ROWS = PAIRS * HALF
SECOND_ROWS = 16
SHARD_ROWS = SECOND_ROWS + FIRST_ROWS
CLASS_ROWS = 160
SIDE = 4
ADJ_ROWS = RELATIONS * CAPACITY
ROWS = KINDS * TARGETS
GRAD_START = ADJ_ROWS + ROWS
DEGREE_START = GRAD_START + UNITS
DEGREE_ROWS = ROWS // 4
GRAPH_ROWS = DEGREE_START + DEGREE_ROWS
MIB = 1024 * 1024


def dot(a, b, contract):
    return lax.dot_general(a, b, ((contract[:1], contract[1:]), ((), ())), preferred_element_type=F32)


def eye(size):
    row = lax.broadcasted_iota(jnp.int32, (size, size), 0)
    column = lax.broadcasted_iota(jnp.int32, (size, size), 1)
    return (row == column).astype(F32).astype(BF16)


def swap_halves(tile):
    return pltpu.roll(tile, UNITS, 1)


def low_half(rows):
    return lax.broadcasted_iota(jnp.int32, (rows, 2 * UNITS), 1) < UNITS


def pack_kernel(core_ref, x_ref, w_ref, out_ref, x_tile, w_tiles, packed_ref, w_sem, x_sem, out_sem):
    load_x = pltpu.make_async_copy(x_ref, x_tile, w_sem.at[PAIRS])
    load_x.start()
    loads = []
    for pair in range(PAIRS):
        loads.append(pltpu.make_async_copy(w_ref.at[2 * pair + core_ref[0]], w_tiles.at[pair], w_sem.at[pair]))
        loads[-1].start()
    load_x.wait()
    stores = []
    for dest in range(FEAT):
        stores.append(pltpu.make_async_copy(x_tile, out_ref.at[dest, :, pl.ds(0, NODES)], x_sem.at[dest]))
        stores[-1].start()
    for load in loads:
        load.wait()
    low = low_half(COLUMNS)
    for tile in range(FEAT // 2):
        lanes = pl.ds(tile * 2 * UNITS, 2 * UNITS)
        first, second, third = [w_tiles[pair, :, lanes].astype(F32) for pair in range(PAIRS)]
        front = pl.ds(0, 2 * UNITS)
        back = pl.ds(2 * UNITS, 2 * UNITS)
        packed_ref[2 * tile, :, front] = jnp.where(low, first, swap_halves(second)).astype(BF16)
        packed_ref[2 * tile, :, back] = third.astype(BF16)
        packed_ref[2 * tile + 1, :, front] = jnp.where(low, swap_halves(first), second).astype(BF16)
        packed_ref[2 * tile + 1, :, back] = swap_halves(third).astype(BF16)
        if tile % 2:
            dests = pl.ds(2 * tile - 2, 4)
            stores.append(
                pltpu.make_async_copy(
                    packed_ref.at[dests],
                    out_ref.at[dests, :, pl.ds(NODES, WEIGHT_LANES)],
                    out_sem.at[tile // 2],
                )
            )
            stores[-1].start()
    for store in stores:
        store.wait()


def live_slots(ids, count):
    node = lax.broadcasted_iota(jnp.int32, (SLOTS, CAPACITY), 1)
    return (ids >= 0) & (ids < count) & (node < count)


def adjacency_kernel(
    counts_ref,
    offsets_ref,
    slots_ref,
    weight_ref,
    upstream_ref,
    adj_ref,
    value_ref,
):
    tile_row = lax.broadcasted_iota(jnp.int32, (16, CAPACITY), 0).astype(F32).astype(BF16)
    one = jnp.ones((16, CAPACITY), BF16)
    zero = jnp.zeros((16, CAPACITY), BF16)
    target = lax.broadcasted_iota(jnp.int32, (TARGETS, CAPACITY), 0)
    place = lax.broadcasted_iota(jnp.int32, (TARGETS, CAPACITY), 1)
    half = CAPACITY // 2
    for group in range(GROUPS):
        count = counts_ref[group]
        pick = (place == target + offsets_ref[group]).astype(F32).astype(BF16)
        adj_ref[group, ADJ_ROWS : ADJ_ROWS + TARGETS, :] = pick

        def relation_step(relation, carry, group=group, count=count, pick=pick):
            ids = slots_ref[group, relation]
            live = live_slots(ids, count)
            origin = pl.multiple_of(relation * CAPACITY, CAPACITY)
            for part in range(2):
                inside = live & (ids >= part * half) & (ids < (part + 1) * half)
                value = jnp.where(inside, ids - part * half, -1).astype(F32)
                for slot in range(SLOTS):
                    value_ref[part, slot] = jnp.broadcast_to(
                        value[slot : slot + 1, :], (16, CAPACITY)
                    ).astype(BF16)
            for part in range(2):

                def tile_step(step, carry, part=part):
                    base = step * 32
                    here = tile_row + base.astype(F32).astype(BF16)
                    there = here + jnp.full((), 16, BF16)
                    first = zero
                    second = zero
                    for slot in range(SLOTS):
                        value = value_ref[part, slot]
                        first = first + jnp.where(value == here, one, zero)
                        second = second + jnp.where(value == there, one, zero)
                    start = pl.multiple_of(origin + part * half + base, 32)
                    adj_ref[group, pl.ds(start, 16), :] = first
                    adj_ref[group, pl.ds(start + 16, 16), :] = second
                    return carry

                lax.fori_loop(0, half // 32, tile_step, 0)
            start = pl.multiple_of(ADJ_ROWS + (relation + 1) * TARGETS, TARGETS)
            adj_ref[group, pl.ds(start, TARGETS), :] = dot(
                pick, adj_ref[group, pl.ds(origin, CAPACITY), :], (1, 1)
            ).astype(BF16)
            return carry

        lax.fori_loop(0, RELATIONS, relation_step, 0)
        rows = adj_ref[group, ADJ_ROWS:GRAD_START, :]
        degree = jnp.maximum(jnp.sum(rows.astype(F32), axis=1, keepdims=True), 1.0)
        for part in range(4):
            piece = degree[part * DEGREE_ROWS : (part + 1) * DEGREE_ROWS]
            adj_ref[group, DEGREE_START:, part * 2 * UNITS : (part + 1) * 2 * UNITS] = jnp.broadcast_to(
                piece, (DEGREE_ROWS, 2 * UNITS)
            ).astype(BF16)
        upstream = upstream_ref[group * TARGETS : (group + 1) * TARGETS, :]
        returned = []
        for kind in range(KINDS):
            returned.append(dot(upstream, weight_ref[kind * UNITS : (kind + 1) * UNITS, :], (1, 1)))
        spread = (jnp.concatenate(returned, axis=0) / degree).astype(BF16)
        adj_ref[group, GRAD_START:DEGREE_START, :] = dot(spread, rows, (0, 0)).astype(BF16)


def layer_kernel(
    core_ref,
    counts_ref,
    message_ref,
    first_ref,
    slots_ref,
    bias_ref,
    weight_ref,
    upstream_ref,
    adj_from,
    keep_ref,
    send_ref,
    score_ref,
    adj_ref,
    adj_sem,
    mixed_ref,
    low_ref,
    high_ref,
    whole_ref,
):
    def fetch(group, relation):
        size = CAPACITY if relation < RELATIONS else GRAPH_ROWS - ADJ_ROWS
        rows = pl.ds(relation * CAPACITY, size)
        return pltpu.make_async_copy(
            adj_from.at[group, rows], adj_ref.at[group, rows], adj_sem.at[group, relation]
        )

    for group in range(GROUPS):
        for relation in range(KINDS):
            fetch(group, relation).start()
    turn = eye(WEIGHT_LANES)
    first_weight = [dot(turn, first_ref[part], (1, 1)).astype(BF16) for part in range(CORES)]
    size = WIDTH // 3
    preacts = []
    for group in range(GROUPS):
        lanes = slice(group * CAPACITY, (group + 1) * CAPACITY)
        count = counts_ref[group]
        for relation in range(RELATIONS):
            fetch(group, relation).wait()
            adjacency = adj_ref[group, relation * CAPACITY : (relation + 1) * CAPACITY, :]
            live = live_slots(slots_ref[group, relation], count)
            inverse = 1.0 / jnp.maximum(jnp.sum(live.astype(F32), axis=0, keepdims=True), 1.0)
            for block in range(3):
                mixed = dot(message_ref[block * size : (block + 1) * size, lanes], adjacency, (1, 0))
                start = relation * WIDTH + block * size
                mixed_ref[group, start : start + size, :] = (mixed * inverse).astype(BF16)
        preact = bias_ref[...] + dot(first_weight[0][:UNITS], message_ref[:, lanes], (1, 0))
        for kind in range(1, KINDS):
            preact = preact + dot(
                first_weight[kind % CORES][kind // CORES * UNITS : (kind // CORES + 1) * UNITS],
                mixed_ref[group, (kind - 1) * WIDTH : kind * WIDTH, :],
                (1, 0),
            )
        preacts.append(preact)
    hiddens = []
    for group, preact in enumerate(preacts):
        fetch(group, RELATIONS).wait()
        hiddens.append(jnp.maximum(preact, 0.0).astype(BF16))
        pre_grad = jnp.where(preact > 0, adj_ref[group, GRAD_START:DEGREE_START, :].astype(F32), 0.0)
        nothing = jnp.zeros_like(pre_grad)
        low_ref[group] = jnp.concatenate([pre_grad, nothing], axis=0).astype(BF16)
        high_ref[group] = jnp.concatenate([nothing, pre_grad], axis=0).astype(BF16)
    score_parts = []
    grad_second = jnp.zeros((CLASSES, KINDS * UNITS), F32)
    for group, hidden in enumerate(hiddens):
        rows = adj_ref[group, ADJ_ROWS:GRAD_START, :]
        degree = adj_ref[group, DEGREE_START:, :].astype(F32)
        degree = jnp.concatenate([degree[:, part * 2 * UNITS : part * 2 * UNITS + UNITS] for part in range(4)], axis=0)
        second_in = dot(rows, hidden, (1, 1)) / degree
        wide = jnp.concatenate(
            [second_in[kind * TARGETS : (kind + 1) * TARGETS] for kind in range(KINDS)], axis=1
        ).astype(BF16)
        score_parts.append(dot(weight_ref[...], wide, (0, 1)))
        upstream = upstream_ref[group * TARGETS : (group + 1) * TARGETS, :]
        grad_second = grad_second + dot(upstream, wide, (0, 0))
    tail = jnp.zeros((CLASS_ROWS - CLASSES, 2 * UNITS), F32)
    score = jnp.concatenate([jnp.concatenate(score_parts, axis=1), tail], axis=0)
    score_ref[...] = score
    for pair in range(PAIRS):
        total = jnp.zeros((WIDTH, 2 * UNITS), F32)
        for group in range(GROUPS):
            lanes = slice(group * CAPACITY, (group + 1) * CAPACITY)
            if pair == 0:
                even = message_ref[:, lanes]
            else:
                even = mixed_ref[group, (2 * pair - 1) * WIDTH : 2 * pair * WIDTH, :]
            odd = mixed_ref[group, 2 * pair * WIDTH : (2 * pair + 1) * WIDTH, :]
            total = total + dot(even, low_ref[group], (1, 1)) + dot(odd, high_ref[group], (1, 1))
        total = total.reshape(FEAT, COLUMNS, 2 * UNITS)
        start = SECOND_ROWS + pair * HALF
        for part in range(CORES):
            whole_ref[part, :, start : start + HALF, :] = total[:, part * HALF : (part + 1) * HALF, :]
    packed = []
    for pair in range(PAIRS):
        packed.append(grad_second[:, pair * 2 * UNITS : (pair + 1) * 2 * UNITS])
        packed.append(tail)
    packed.append(jnp.zeros((Z * CORES * SECOND_ROWS - PAIRS * CLASS_ROWS, 2 * UNITS), F32))
    packed = jnp.concatenate(packed, axis=0).reshape(Z, CORES, SECOND_ROWS, 2 * UNITS)
    for part in range(CORES):
        whole_ref[part, :, :SECOND_ROWS, :] = packed[:, part]
    core = core_ref[0]
    keep_ref[...] = whole_ref[core]
    send_ref[...] = whole_ref[1 - core].astype(BF16)


def merge_kernel(core_ref, keep_ref, both_ref, message_ref, second_ref):
    chip = keep_ref[...] + both_ref[1 - core_ref[0]].astype(F32)
    message_ref[...] = chip[:, SECOND_ROWS:, :].astype(BF16)
    second_ref[...] = chip[:, :SECOND_ROWS, :].astype(BF16)


def relay_kernel(message_ref, second_ref, score_ref, shards_ref, passed_ref):
    shards_ref[:, SECOND_ROWS:, :] = message_ref[...]
    shards_ref[:, :SECOND_ROWS, :] = second_ref[...]
    passed_ref[...] = score_ref[...]


def fold_kernel(pieces_ref, s0_ref, s1_ref, s2_ref, s3_ref, copies_ref, score_ref):
    total = pieces_ref[0].astype(F32)
    for part in range(1, Z):
        total = total + pieces_ref[part].astype(F32)
    total = total.astype(BF16)
    for part in range(BLOCKS):
        copies_ref[part] = total
    score_ref[...] = s0_ref[...] + s1_ref[...] + s2_ref[...] + s3_ref[...]


def unpack_kernel(shards_ref, s0_ref, s1_ref, s2_ref, s3_ref, first_ref, second_ref, logits_ref):
    low = low_half(HALF)
    for tile in range(FEAT // 2):
        lanes = pl.ds(tile * 2 * UNITS, 2 * UNITS)
        for part in range(CORES):
            left = shards_ref[part, tile].astype(F32)
            right = shards_ref[CORES + part, tile].astype(F32)
            rows = pl.ds(part * HALF, HALF)
            for pair in range(PAIRS):
                start = SECOND_ROWS + pair * HALF
                a = left[start : start + HALF]
                b = right[start : start + HALF]
                first_ref[2 * pair, rows, lanes] = jnp.where(low, a, swap_halves(b))
                first_ref[2 * pair + 1, rows, lanes] = jnp.where(low, swap_halves(a), b)
    packed = jnp.stack([shards_ref[part, :, :SECOND_ROWS, :] for part in range(BLOCK)], axis=1)
    packed = packed.reshape(Z * CORES * SECOND_ROWS, 2 * UNITS)
    identity = eye(2 * UNITS)
    for pair in range(PAIRS):
        block = packed[pair * CLASS_ROWS : (pair + 1) * CLASS_ROWS]
        turned = dot(identity, block, (1, 1))
        second_ref[2 * pair] = turned[:UNITS, :CLASSES]
        second_ref[2 * pair + 1] = turned[UNITS:, :CLASSES]
    logits_ref[...] = (s0_ref[...] + s1_ref[...] + s2_ref[...] + s3_ref[...])[:CLASSES]


VMEM = pl.BlockSpec(memory_space=pltpu.VMEM)
SMEM = pl.BlockSpec(memory_space=pltpu.SMEM)


def params(mib):
    return pltpu.CompilerParams(vmem_limit_bytes=mib * MIB)


def cost(flops, size):
    return pl.CostEstimate(flops=flops, bytes_accessed=size, transcendentals=0)


def shape(*dims, dtype=BF16):
    return jax.ShapeDtypeStruct(dims, dtype)


def pack(core, x, w):
    anywhere = pl.BlockSpec(memory_space=pl.ANY)
    return pl.pallas_call(
        pack_kernel,
        out_shape=shape(FEAT, COLUMNS, MESSAGE),
        in_specs=[SMEM, anywhere, anywhere],
        out_specs=anywhere,
        scratch_shapes=[
            pltpu.VMEM((COLUMNS, NODES), BF16),
            pltpu.VMEM((PAIRS, COLUMNS, HIDDEN), BF16),
            pltpu.VMEM((FEAT, COLUMNS, WEIGHT_LANES), BF16),
            pltpu.SemaphoreType.DMA((PAIRS + 1,)),
            pltpu.SemaphoreType.DMA((FEAT,)),
            pltpu.SemaphoreType.DMA((FEAT // 4,)),
        ],
        compiler_params=params(58),
    )(core, x, w)


def adjacency(counts, offsets, slots, weight, upstream):
    return pl.pallas_call(
        adjacency_kernel,
        out_shape=shape(GROUPS, GRAPH_ROWS, CAPACITY),
        in_specs=[SMEM] * 2 + [VMEM] * 3,
        out_specs=VMEM,
        scratch_shapes=[pltpu.VMEM((2, SLOTS, 16, CAPACITY), BF16)],
        compiler_params=params(58),
        cost_estimate=cost(8 * 10**9, 8 * MIB),
    )(counts, offsets, slots, weight, upstream)


def layers(core, counts, message, first, slots, bias, weight, upstream, adj):
    shard = shape(Z, SHARD_ROWS, 2 * UNITS, dtype=F32)
    return pl.pallas_call(
        layer_kernel,
        out_shape=(shard, shape(Z, SHARD_ROWS, 2 * UNITS), shape(CLASS_ROWS, GROUPS * TARGETS, dtype=F32)),
        in_specs=[SMEM] * 2 + [VMEM] * 6 + [pl.BlockSpec(memory_space=pl.ANY)],
        out_specs=(VMEM, VMEM, VMEM),
        scratch_shapes=[
            pltpu.VMEM(adj.shape, BF16),
            pltpu.SemaphoreType.DMA((GROUPS, KINDS)),
            pltpu.VMEM((GROUPS, RELATIONS * WIDTH, CAPACITY), BF16),
            pltpu.VMEM((GROUPS, 2 * UNITS, CAPACITY), BF16),
            pltpu.VMEM((GROUPS, 2 * UNITS, CAPACITY), BF16),
            pltpu.VMEM((CORES, Z, SHARD_ROWS, 2 * UNITS), F32),
        ],
        compiler_params=params(44),
        cost_estimate=cost(12 * 10**9, 12 * MIB),
    )(core, counts, message, first, slots, bias, weight, upstream, adj)


def merge(core, keep, both):
    return pl.pallas_call(
        merge_kernel,
        out_shape=(shape(FEAT, FIRST_ROWS, 2 * UNITS), shape(Z, SECOND_ROWS, 2 * UNITS)),
        in_specs=[SMEM] + [VMEM] * 2,
        out_specs=(VMEM,) * 2,
        compiler_params=params(8),
    )(core, keep, both)


def relay(message, second, score):
    return pl.pallas_call(
        relay_kernel,
        out_shape=(shape(Z, SHARD_ROWS, 2 * UNITS), shape(*score.shape, dtype=F32)),
        in_specs=[VMEM] * 3,
        out_specs=(VMEM,) * 2,
        compiler_params=params(8),
    )(message, second, score)


def fold(pieces, scores):
    return pl.pallas_call(
        fold_kernel,
        out_shape=(shape(BLOCKS, SHARD_ROWS, 2 * UNITS), shape(*scores[0].shape, dtype=F32)),
        in_specs=[VMEM] * 5,
        out_specs=(VMEM,) * 2,
        compiler_params=params(8),
    )(pieces, *scores)


def row_hops(step):
    return [(i, i // SIDE * SIDE + (i + step) % SIDE) for i in range(FEAT)]


def column_hops(step):
    return [(i, (i + step * SIDE) % FEAT) for i in range(FEAT)]


def spread_out(score, hops):
    return [score] + [lax.ppermute(score, "feat", hops(step)) for step in range(1, SIDE)]


def unpack(shards, scores):
    return pl.pallas_call(
        unpack_kernel,
        out_shape=(
            shape(KINDS, COLUMNS, HIDDEN, dtype=F32),
            shape(KINDS, UNITS, CLASSES, dtype=F32),
            shape(CLASSES, GROUPS * TARGETS, dtype=F32),
        ),
        in_specs=[VMEM] * 5,
        out_specs=(VMEM, VMEM, VMEM),
        compiler_params=params(8),
    )(shards, *scores)


def local(
    vertex_embeddings,
    adjacent_vertices,
    node_counts,
    target_offsets,
    weight_one,
    bias_one,
    weight_two,
    score_derivative,
):
    core = (lax.axis_index("batch") % CORES).astype(jnp.int32).reshape(1)
    chips = [[z * CORES + c for c in range(CORES)] for z in range(Z)]
    same_core = [[z * CORES + c for z in range(Z)] for c in range(CORES)]
    message = lax.all_to_all(pack(core, vertex_embeddings.T, weight_one), "feat", 0, 0)
    message = message.reshape(WIDTH, MESSAGE)
    first = lax.all_gather(message[:, NODES:], "batch", axis_index_groups=chips)
    slots = jnp.swapaxes(adjacent_vertices, 2, 3)
    weight = weight_two.reshape(KINDS * UNITS, CLASSES)
    adj = adjacency(node_counts, target_offsets, slots, weight, score_derivative)
    keep, send, score = layers(
        core,
        node_counts,
        message,
        first,
        slots,
        bias_one.reshape(UNITS, 1),
        weight,
        score_derivative,
        adj,
    )
    both = lax.all_gather(send, "batch", axis_index_groups=chips)
    message, second = merge(core, keep, both)
    message = lax.all_to_all(message, "feat", 0, 0)
    shards, score = relay(message, second, score)
    pieces = lax.all_to_all(shards, "batch", 0, 0, axis_index_groups=same_core)
    copies, score = fold(pieces, spread_out(score, row_hops))
    blocks = [[block * BLOCK + i for i in range(BLOCK)] for block in range(BLOCKS)]
    same_place = [[block * BLOCK + i for block in range(BLOCKS)] for i in range(BLOCK)]
    shards = lax.all_to_all(copies, "batch", 0, 0, axis_index_groups=same_place)
    scores = spread_out(score, column_hops)
    shards = lax.all_gather(shards, "batch", axis_index_groups=blocks)
    first_grad, second_grad, logits = unpack(shards, scores)
    return (logits.T, first_grad, second_grad)


def solution(mesh):
    placed = (
        P("batch", "feat"),
        P("batch", None, None, None),
        P("batch"),
        P("batch"),
        P(None, "feat", None),
        P("feat"),
        P(None, "feat", None),
        P("batch", None),
    )
    return jax.shard_map(
        local,
        mesh=mesh,
        in_specs=placed,
        out_specs=(P("batch", None), P(None, "feat", None), P(None, "feat", None)),
        check_vma=False,
    )
```

```python
import jax
import jax.numpy as jnp
from jax import lax
from jax.experimental import pallas as pl
from jax.experimental.pallas import tpu as pltpu
from jax.sharding import PartitionSpec as P

BF16 = jnp.bfloat16
F32 = jnp.float32

GROUPS = 2
CAPACITY = 512
RELATIONS = 5
KINDS = RELATIONS + 1
SLOTS = 8
TARGETS = 64
CLASSES = 153
FEAT = 16
COLUMNS = 48
WIDTH = FEAT * COLUMNS
UNITS = 64
HIDDEN = FEAT * UNITS
PAIRS = KINDS // 2
NODES = GROUPS * CAPACITY
WEIGHT_LANES = 256
MESSAGE = NODES + WEIGHT_LANES
Z = 16
CORES = 2
BLOCK = 2 * CORES
BLOCKS = Z * CORES // BLOCK
HALF = COLUMNS // CORES
FIRST_ROWS = PAIRS * HALF
SECOND_ROWS = 16
SHARD_ROWS = SECOND_ROWS + FIRST_ROWS
CLASS_ROWS = 160
SIDE = 4
ADJ_ROWS = RELATIONS * CAPACITY
ROWS = KINDS * TARGETS
GRAD_START = ADJ_ROWS + ROWS
DEGREE_START = GRAD_START + UNITS
DEGREE_ROWS = ROWS // 4
GRAPH_ROWS = DEGREE_START + DEGREE_ROWS
MIB = 1024 * 1024


def dot(a, b, contract):
    return lax.dot_general(a, b, ((contract[:1], contract[1:]), ((), ())), preferred_element_type=F32)


def eye(size):
    row = lax.broadcasted_iota(jnp.int32, (size, size), 0)
    column = lax.broadcasted_iota(jnp.int32, (size, size), 1)
    return (row == column).astype(F32).astype(BF16)


def swap_halves(tile):
    return pltpu.roll(tile, UNITS, 1)


def low_half(rows):
    return lax.broadcasted_iota(jnp.int32, (rows, 2 * UNITS), 1) < UNITS


def pack_kernel(core_ref, x_ref, w_ref, out_ref, x_tile, w_tiles, packed_ref, w_sem, x_sem, out_sem):
    load_x = pltpu.make_async_copy(x_ref, x_tile, w_sem.at[PAIRS])
    load_x.start()
    loads = []
    for pair in range(PAIRS):
        loads.append(pltpu.make_async_copy(w_ref.at[2 * pair + core_ref[0]], w_tiles.at[pair], w_sem.at[pair]))
        loads[-1].start()
    load_x.wait()
    stores = []
    for dest in range(FEAT):
        stores.append(pltpu.make_async_copy(x_tile, out_ref.at[dest, :, pl.ds(0, NODES)], x_sem.at[dest]))
        stores[-1].start()
    for load in loads:
        load.wait()
    low = low_half(COLUMNS)
    for tile in range(FEAT // 2):
        lanes = pl.ds(tile * 2 * UNITS, 2 * UNITS)
        first, second, third = [w_tiles[pair, :, lanes].astype(F32) for pair in range(PAIRS)]
        front = pl.ds(0, 2 * UNITS)
        back = pl.ds(2 * UNITS, 2 * UNITS)
        packed_ref[2 * tile, :, front] = jnp.where(low, first, swap_halves(second)).astype(BF16)
        packed_ref[2 * tile, :, back] = third.astype(BF16)
        packed_ref[2 * tile + 1, :, front] = jnp.where(low, swap_halves(first), second).astype(BF16)
        packed_ref[2 * tile + 1, :, back] = swap_halves(third).astype(BF16)
    stores.append(pltpu.make_async_copy(packed_ref, out_ref.at[:, :, pl.ds(NODES, WEIGHT_LANES)], out_sem))
    stores[-1].start()
    for store in stores:
        store.wait()


def live_slots(ids, count):
    node = lax.broadcasted_iota(jnp.int32, (SLOTS, CAPACITY), 1)
    return (ids >= 0) & (ids < count) & (node < count)


def adjacency_kernel(
    counts_ref,
    offsets_ref,
    slots_ref,
    weight_ref,
    upstream_ref,
    adj_ref,
    value_ref,
):
    tile_row = lax.broadcasted_iota(jnp.int32, (16, CAPACITY), 0).astype(F32).astype(BF16)
    one = jnp.ones((16, CAPACITY), BF16)
    zero = jnp.zeros((16, CAPACITY), BF16)
    target = lax.broadcasted_iota(jnp.int32, (TARGETS, CAPACITY), 0)
    place = lax.broadcasted_iota(jnp.int32, (TARGETS, CAPACITY), 1)
    half = CAPACITY // 2
    for group in range(GROUPS):
        count = counts_ref[group]
        pick = (place == target + offsets_ref[group]).astype(F32).astype(BF16)
        adj_ref[group, ADJ_ROWS : ADJ_ROWS + TARGETS, :] = pick

        def relation_step(relation, carry, group=group, count=count, pick=pick):
            ids = slots_ref[group, relation]
            live = live_slots(ids, count)
            origin = pl.multiple_of(relation * CAPACITY, CAPACITY)
            for part in range(2):
                inside = live & (ids >= part * half) & (ids < (part + 1) * half)
                value = jnp.where(inside, ids - part * half, -1).astype(F32)
                for slot in range(SLOTS):
                    value_ref[part, slot] = jnp.broadcast_to(
                        value[slot : slot + 1, :], (16, CAPACITY)
                    ).astype(BF16)
            for part in range(2):

                def tile_step(step, carry, part=part):
                    base = step * 32
                    here = tile_row + base.astype(F32).astype(BF16)
                    there = here + jnp.full((), 16, BF16)
                    first = zero
                    second = zero
                    for slot in range(SLOTS):
                        value = value_ref[part, slot]
                        first = first + jnp.where(value == here, one, zero)
                        second = second + jnp.where(value == there, one, zero)
                    start = pl.multiple_of(origin + part * half + base, 32)
                    adj_ref[group, pl.ds(start, 16), :] = first
                    adj_ref[group, pl.ds(start + 16, 16), :] = second
                    return carry

                lax.fori_loop(0, half // 32, tile_step, 0)
            start = pl.multiple_of(ADJ_ROWS + (relation + 1) * TARGETS, TARGETS)
            adj_ref[group, pl.ds(start, TARGETS), :] = dot(
                pick, adj_ref[group, pl.ds(origin, CAPACITY), :], (1, 1)
            ).astype(BF16)
            return carry

        lax.fori_loop(0, RELATIONS, relation_step, 0)
        rows = adj_ref[group, ADJ_ROWS:GRAD_START, :]
        degree = jnp.maximum(jnp.sum(rows.astype(F32), axis=1, keepdims=True), 1.0)
        for part in range(4):
            piece = degree[part * DEGREE_ROWS : (part + 1) * DEGREE_ROWS]
            adj_ref[group, DEGREE_START:, part * 2 * UNITS : (part + 1) * 2 * UNITS] = jnp.broadcast_to(
                piece, (DEGREE_ROWS, 2 * UNITS)
            ).astype(BF16)
        upstream = upstream_ref[group * TARGETS : (group + 1) * TARGETS, :]
        returned = []
        for kind in range(KINDS):
            returned.append(dot(upstream, weight_ref[kind * UNITS : (kind + 1) * UNITS, :], (1, 1)))
        spread = (jnp.concatenate(returned, axis=0) / degree).astype(BF16)
        adj_ref[group, GRAD_START:DEGREE_START, :] = dot(spread, rows, (0, 0)).astype(BF16)


def layer_kernel(
    core_ref,
    counts_ref,
    message_ref,
    first_ref,
    slots_ref,
    bias_ref,
    weight_ref,
    upstream_ref,
    adj_from,
    keep_ref,
    send_ref,
    score_ref,
    adj_ref,
    adj_sem,
    mixed_ref,
    low_ref,
    high_ref,
    whole_ref,
):
    def fetch(group, relation):
        size = CAPACITY if relation < RELATIONS else GRAPH_ROWS - ADJ_ROWS
        rows = pl.ds(relation * CAPACITY, size)
        return pltpu.make_async_copy(
            adj_from.at[group, rows], adj_ref.at[group, rows], adj_sem.at[group, relation]
        )

    for group in range(GROUPS):
        for relation in range(KINDS):
            fetch(group, relation).start()
    turn = eye(WEIGHT_LANES)
    first_weight = [dot(turn, first_ref[part], (1, 1)).astype(BF16) for part in range(CORES)]
    size = WIDTH // 3
    preacts = []
    for group in range(GROUPS):
        lanes = slice(group * CAPACITY, (group + 1) * CAPACITY)
        count = counts_ref[group]
        for relation in range(RELATIONS):
            fetch(group, relation).wait()
            adjacency = adj_ref[group, relation * CAPACITY : (relation + 1) * CAPACITY, :]
            live = live_slots(slots_ref[group, relation], count)
            inverse = 1.0 / jnp.maximum(jnp.sum(live.astype(F32), axis=0, keepdims=True), 1.0)
            for block in range(3):
                mixed = dot(message_ref[block * size : (block + 1) * size, lanes], adjacency, (1, 0))
                start = relation * WIDTH + block * size
                mixed_ref[group, start : start + size, :] = (mixed * inverse).astype(BF16)
        preact = bias_ref[...] + dot(first_weight[0][:UNITS], message_ref[:, lanes], (1, 0))
        for kind in range(1, KINDS):
            preact = preact + dot(
                first_weight[kind % CORES][kind // CORES * UNITS : (kind // CORES + 1) * UNITS],
                mixed_ref[group, (kind - 1) * WIDTH : kind * WIDTH, :],
                (1, 0),
            )
        preacts.append(preact)
    hiddens = []
    for group, preact in enumerate(preacts):
        fetch(group, RELATIONS).wait()
        hiddens.append(jnp.maximum(preact, 0.0).astype(BF16))
        pre_grad = jnp.where(preact > 0, adj_ref[group, GRAD_START:DEGREE_START, :].astype(F32), 0.0)
        nothing = jnp.zeros_like(pre_grad)
        low_ref[group] = jnp.concatenate([pre_grad, nothing], axis=0).astype(BF16)
        high_ref[group] = jnp.concatenate([nothing, pre_grad], axis=0).astype(BF16)
    score_parts = []
    grad_second = jnp.zeros((CLASSES, KINDS * UNITS), F32)
    for group, hidden in enumerate(hiddens):
        rows = adj_ref[group, ADJ_ROWS:GRAD_START, :]
        degree = adj_ref[group, DEGREE_START:, :].astype(F32)
        degree = jnp.concatenate([degree[:, part * 2 * UNITS : part * 2 * UNITS + UNITS] for part in range(4)], axis=0)
        second_in = dot(rows, hidden, (1, 1)) / degree
        wide = jnp.concatenate(
            [second_in[kind * TARGETS : (kind + 1) * TARGETS] for kind in range(KINDS)], axis=1
        ).astype(BF16)
        score_parts.append(dot(weight_ref[...], wide, (0, 1)))
        upstream = upstream_ref[group * TARGETS : (group + 1) * TARGETS, :]
        grad_second = grad_second + dot(upstream, wide, (0, 0))
    tail = jnp.zeros((CLASS_ROWS - CLASSES, 2 * UNITS), F32)
    score = jnp.concatenate([jnp.concatenate(score_parts, axis=1), tail], axis=0)
    score_ref[...] = score
    for pair in range(PAIRS):
        total = jnp.zeros((WIDTH, 2 * UNITS), F32)
        for group in range(GROUPS):
            lanes = slice(group * CAPACITY, (group + 1) * CAPACITY)
            if pair == 0:
                even = message_ref[:, lanes]
            else:
                even = mixed_ref[group, (2 * pair - 1) * WIDTH : 2 * pair * WIDTH, :]
            odd = mixed_ref[group, 2 * pair * WIDTH : (2 * pair + 1) * WIDTH, :]
            total = total + dot(even, low_ref[group], (1, 1)) + dot(odd, high_ref[group], (1, 1))
        total = total.reshape(FEAT, COLUMNS, 2 * UNITS)
        start = SECOND_ROWS + pair * HALF
        for part in range(CORES):
            whole_ref[part, :, start : start + HALF, :] = total[:, part * HALF : (part + 1) * HALF, :]
    packed = []
    for pair in range(PAIRS):
        packed.append(grad_second[:, pair * 2 * UNITS : (pair + 1) * 2 * UNITS])
        packed.append(tail)
    packed.append(jnp.zeros((Z * CORES * SECOND_ROWS - PAIRS * CLASS_ROWS, 2 * UNITS), F32))
    packed = jnp.concatenate(packed, axis=0).reshape(Z, CORES, SECOND_ROWS, 2 * UNITS)
    for part in range(CORES):
        whole_ref[part, :, :SECOND_ROWS, :] = packed[:, part]
    core = core_ref[0]
    keep_ref[...] = whole_ref[core]
    send_ref[...] = whole_ref[1 - core].astype(BF16)


def merge_kernel(core_ref, keep_ref, both_ref, message_ref, second_ref):
    chip = keep_ref[...] + both_ref[1 - core_ref[0]].astype(F32)
    message_ref[...] = chip[:, SECOND_ROWS:, :].astype(BF16)
    second_ref[...] = chip[:, :SECOND_ROWS, :].astype(BF16)


def relay_kernel(message_ref, second_ref, score_ref, shards_ref, passed_ref):
    shards_ref[:, SECOND_ROWS:, :] = message_ref[...]
    shards_ref[:, :SECOND_ROWS, :] = second_ref[...]
    passed_ref[...] = score_ref[...]


def fold_kernel(pieces_ref, s0_ref, s1_ref, s2_ref, s3_ref, copies_ref, score_ref):
    total = pieces_ref[0].astype(F32)
    for part in range(1, Z):
        total = total + pieces_ref[part].astype(F32)
    total = total.astype(BF16)
    for part in range(BLOCKS):
        copies_ref[part] = total
    score_ref[...] = s0_ref[...] + s1_ref[...] + s2_ref[...] + s3_ref[...]


def unpack_kernel(shards_ref, s0_ref, s1_ref, s2_ref, s3_ref, first_ref, second_ref, logits_ref):
    low = low_half(HALF)
    for tile in range(FEAT // 2):
        lanes = pl.ds(tile * 2 * UNITS, 2 * UNITS)
        for part in range(CORES):
            left = shards_ref[part, tile].astype(F32)
            right = shards_ref[CORES + part, tile].astype(F32)
            rows = pl.ds(part * HALF, HALF)
            for pair in range(PAIRS):
                start = SECOND_ROWS + pair * HALF
                a = left[start : start + HALF]
                b = right[start : start + HALF]
                first_ref[2 * pair, rows, lanes] = jnp.where(low, a, swap_halves(b))
                first_ref[2 * pair + 1, rows, lanes] = jnp.where(low, swap_halves(a), b)
    packed = jnp.stack([shards_ref[part, :, :SECOND_ROWS, :] for part in range(BLOCK)], axis=1)
    packed = packed.reshape(Z * CORES * SECOND_ROWS, 2 * UNITS)
    identity = eye(2 * UNITS)
    for pair in range(PAIRS):
        block = packed[pair * CLASS_ROWS : (pair + 1) * CLASS_ROWS]
        turned = dot(identity, block, (1, 1))
        second_ref[2 * pair] = turned[:UNITS, :CLASSES]
        second_ref[2 * pair + 1] = turned[UNITS:, :CLASSES]
    logits_ref[...] = (s0_ref[...] + s1_ref[...] + s2_ref[...] + s3_ref[...])[:CLASSES]


VMEM = pl.BlockSpec(memory_space=pltpu.VMEM)
SMEM = pl.BlockSpec(memory_space=pltpu.SMEM)


def params(mib):
    return pltpu.CompilerParams(vmem_limit_bytes=mib * MIB)


def cost(flops, size):
    return pl.CostEstimate(flops=flops, bytes_accessed=size, transcendentals=0)


def shape(*dims, dtype=BF16):
    return jax.ShapeDtypeStruct(dims, dtype)


def pack(core, x, w):
    anywhere = pl.BlockSpec(memory_space=pl.ANY)
    return pl.pallas_call(
        pack_kernel,
        out_shape=shape(FEAT, COLUMNS, MESSAGE),
        in_specs=[SMEM, anywhere, anywhere],
        out_specs=anywhere,
        scratch_shapes=[
            pltpu.VMEM((COLUMNS, NODES), BF16),
            pltpu.VMEM((PAIRS, COLUMNS, HIDDEN), BF16),
            pltpu.VMEM((FEAT, COLUMNS, WEIGHT_LANES), BF16),
            pltpu.SemaphoreType.DMA((PAIRS + 1,)),
            pltpu.SemaphoreType.DMA((FEAT,)),
            pltpu.SemaphoreType.DMA,
        ],
        compiler_params=params(58),
    )(core, x, w)


def adjacency(counts, offsets, slots, weight, upstream):
    return pl.pallas_call(
        adjacency_kernel,
        out_shape=shape(GROUPS, GRAPH_ROWS, CAPACITY),
        in_specs=[SMEM] * 2 + [VMEM] * 3,
        out_specs=VMEM,
        scratch_shapes=[pltpu.VMEM((2, SLOTS, 16, CAPACITY), BF16)],
        compiler_params=params(58),
        cost_estimate=cost(8 * 10**9, 8 * MIB),
    )(counts, offsets, slots, weight, upstream)


def layers(core, counts, message, first, slots, bias, weight, upstream, adj):
    shard = shape(Z, SHARD_ROWS, 2 * UNITS, dtype=F32)
    return pl.pallas_call(
        layer_kernel,
        out_shape=(shard, shape(Z, SHARD_ROWS, 2 * UNITS), shape(CLASS_ROWS, GROUPS * TARGETS, dtype=F32)),
        in_specs=[SMEM] * 2 + [VMEM] * 6 + [pl.BlockSpec(memory_space=pl.ANY)],
        out_specs=(VMEM, VMEM, VMEM),
        scratch_shapes=[
            pltpu.VMEM(adj.shape, BF16),
            pltpu.SemaphoreType.DMA((GROUPS, KINDS)),
            pltpu.VMEM((GROUPS, RELATIONS * WIDTH, CAPACITY), BF16),
            pltpu.VMEM((GROUPS, 2 * UNITS, CAPACITY), BF16),
            pltpu.VMEM((GROUPS, 2 * UNITS, CAPACITY), BF16),
            pltpu.VMEM((CORES, Z, SHARD_ROWS, 2 * UNITS), F32),
        ],
        compiler_params=params(44),
        cost_estimate=cost(12 * 10**9, 12 * MIB),
    )(core, counts, message, first, slots, bias, weight, upstream, adj)


def merge(core, keep, both):
    return pl.pallas_call(
        merge_kernel,
        out_shape=(shape(FEAT, FIRST_ROWS, 2 * UNITS), shape(Z, SECOND_ROWS, 2 * UNITS)),
        in_specs=[SMEM] + [VMEM] * 2,
        out_specs=(VMEM,) * 2,
        compiler_params=params(8),
    )(core, keep, both)


def relay(message, second, score):
    return pl.pallas_call(
        relay_kernel,
        out_shape=(shape(Z, SHARD_ROWS, 2 * UNITS), shape(*score.shape, dtype=F32)),
        in_specs=[VMEM] * 3,
        out_specs=(VMEM,) * 2,
        compiler_params=params(8),
    )(message, second, score)


def fold(pieces, scores):
    return pl.pallas_call(
        fold_kernel,
        out_shape=(shape(BLOCKS, SHARD_ROWS, 2 * UNITS), shape(*scores[0].shape, dtype=F32)),
        in_specs=[VMEM] * 5,
        out_specs=(VMEM,) * 2,
        compiler_params=params(8),
    )(pieces, *scores)


def row_hops(step):
    return [(i, i // SIDE * SIDE + (i + step) % SIDE) for i in range(FEAT)]


def column_hops(step):
    return [(i, (i + step * SIDE) % FEAT) for i in range(FEAT)]


def spread_out(score, hops):
    sent = score.astype(BF16)
    return [score] + [lax.ppermute(sent, "feat", hops(step)) for step in range(1, SIDE)]


def unpack(shards, scores):
    return pl.pallas_call(
        unpack_kernel,
        out_shape=(
            shape(KINDS, COLUMNS, HIDDEN, dtype=F32),
            shape(KINDS, UNITS, CLASSES, dtype=F32),
            shape(CLASSES, GROUPS * TARGETS, dtype=F32),
        ),
        in_specs=[VMEM] * 5,
        out_specs=(VMEM, VMEM, VMEM),
        compiler_params=params(8),
    )(shards, *scores)


def local(
    vertex_embeddings,
    adjacent_vertices,
    node_counts,
    target_offsets,
    weight_one,
    bias_one,
    weight_two,
    score_derivative,
):
    core = (lax.axis_index("batch") % CORES).astype(jnp.int32).reshape(1)
    chips = [[z * CORES + c for c in range(CORES)] for z in range(Z)]
    same_core = [[z * CORES + c for z in range(Z)] for c in range(CORES)]
    message = lax.all_to_all(pack(core, vertex_embeddings.T, weight_one), "feat", 0, 0)
    message = message.reshape(WIDTH, MESSAGE)
    first = lax.all_gather(message[:, NODES:], "batch", axis_index_groups=chips)
    slots = jnp.swapaxes(adjacent_vertices, 2, 3)
    weight = weight_two.reshape(KINDS * UNITS, CLASSES)
    adj = adjacency(node_counts, target_offsets, slots, weight, score_derivative)
    keep, send, score = layers(
        core,
        node_counts,
        message,
        first,
        slots,
        bias_one.reshape(UNITS, 1),
        weight,
        score_derivative,
        adj,
    )
    both = lax.all_gather(send, "batch", axis_index_groups=chips)
    message, second = merge(core, keep, both)
    message = lax.all_to_all(message, "feat", 0, 0)
    shards, score = relay(message, second, score)
    pieces = lax.all_to_all(shards, "batch", 0, 0, axis_index_groups=same_core)
    copies, score = fold(pieces, spread_out(score, row_hops))
    blocks = [[block * BLOCK + i for i in range(BLOCK)] for block in range(BLOCKS)]
    same_place = [[block * BLOCK + i for block in range(BLOCKS)] for i in range(BLOCK)]
    shards = lax.all_to_all(copies, "batch", 0, 0, axis_index_groups=same_place)
    scores = spread_out(score, column_hops)
    shards = lax.all_gather(shards, "batch", axis_index_groups=blocks)
    first_grad, second_grad, logits = unpack(shards, scores)
    return (logits.T, first_grad, second_grad)


def solution(mesh):
    placed = (
        P("batch", "feat"),
        P("batch", None, None, None),
        P("batch"),
        P("batch"),
        P(None, "feat", None),
        P("feat"),
        P(None, "feat", None),
        P("batch", None),
    )
    return jax.shard_map(
        local,
        mesh=mesh,
        in_specs=placed,
        out_specs=(P("batch", None), P(None, "feat", None), P(None, "feat", None)),
        check_vma=False,
    )
```
